32 devices in a mesh: dp: 4 (over y, x), tensor: 8 (over z, core).
Axes of the slice: x: 2, y: 2, z: 4, core: 2. Of those that a mesh axis runs over, the one named last changes fastest.
Arguments:
- images: bfloat16 [8192, 768], P('dp'), may hold values from -6 to 6
- head: bfloat16 [768, 768], P(None, 'tensor'), may hold values from -0.21875 to 0.21875
- tea_img: bfloat16 [8192, 1536], P('dp'), may hold values from -6 to 6
- stu_txt: bfloat16 [8192, 768], P(('dp', 'tensor')), may hold values from -6 to 6
- tea_txt: bfloat16 [8192, 1536], P(('dp', 'tensor')), may hold values from -6 to 6
Outputs:
- grad_images: float32 [8192, 768], P(('dp', 'tensor'))
- grad_head: float32 [768, 768], P(None, 'tensor')
- grad_text: float32 [8192, 768], P(('dp', 'tensor'))
The draws below stay inside these ranges and needn't reach their ends.
All inputs are finite; a program needn't handle non-finite values.
Results may differ from the reference program's by a relative error of at most 0.012.
Values may be sent and summed in bfloat16 or wider, within the bound.
No kernel may reach another device: no remote copies, remote signals or barrier semaphores. Data moves between devices by JAX's collectives and lax.ppermute only.
A program may use at most 192 MiB of HBM per device.

```python
import math
import jax
import jax.numpy as jnp
from jax import lax

D_STU = 768
EMB = 768
D_TEA = 1536
PAIRS = 8192


def block_levels(key, shape, cuts, smallest, largest):
    factor_of, own = 1.0, jax.random.fold_in(key, 6)
    for dim, parts in cuts:
        heights = jnp.exp(jax.random.uniform(jax.random.fold_in(own, dim), (parts,), jnp.float32, smallest / len(cuts), largest / len(cuts)))
        factor_of = factor_of * jnp.repeat(heights, shape[dim] // parts).reshape([-1 if axis == dim else 1 for axis in range(len(shape))])
    return factor_of


def scatter_about(own_key, shape, scale, reach, cuts=(), kind=jnp.bfloat16):
    values = scale * jax.random.normal(own_key, shape, jnp.float32)
    if cuts:
        values = values * block_levels(own_key, shape, cuts, -0.22, 0.18)
    return jnp.clip(values, -reach, reach).astype(kind)


def setup_inputs(seed: int = 0) -> dict:
    splits = jax.random.split(jax.random.key(seed), 6)
    return {
        "images": scatter_about(splits[0], (PAIRS, D_STU), 1.0, 6.0, ((0, 4),)),
        "head": scatter_about(splits[1], (D_STU, EMB), D_STU ** -0.5, 0.21875, ((1, 8),)),
        "tea_img": scatter_about(splits[2], (PAIRS, D_TEA), 1.0, 6.0, ((0, 4),)),
        "stu_txt": scatter_about(splits[3], (PAIRS, EMB), 1.0, 6.0, ((0, 32),)),
        "tea_txt": scatter_about(splits[4], (PAIRS, D_TEA), 1.0, 6.0, ((0, 32),)),
    }


logit_scale = 64.0
logit_bias = -2.0
loss_scale = 65536.0

def normalize(values):
    floats = values.astype(jnp.float32)
    length = jnp.sqrt(lax.optimization_barrier(jnp.sum(floats * floats, axis=1, keepdims=True)) + 1e-06)
    return (floats / length, length)

def affinity_tile(img_emb, tea_img_emb, txt_piece, tea_piece, factor):
    contract = (((1,), (1,)), ((), ()))
    target = jax.nn.sigmoid(logit_scale * lax.dot_general(tea_img_emb, tea_piece, contract, preferred_element_type=jnp.float32) + logit_bias)
    student = logit_scale * lax.dot_general(img_emb, txt_piece, contract, preferred_element_type=jnp.float32) + logit_bias
    return ((jax.nn.sigmoid(student) - target) * factor).astype(jnp.bfloat16)

def reference(images, head, tea_img, stu_txt, tea_txt):
    pair_count = images.shape[0]
    emb_width = head.shape[1]
    factor = logit_scale * loss_scale / pair_count
    proj = jnp.dot(images, head, preferred_element_type=jnp.float32).astype(jnp.bfloat16)
    img_unit, proj_norm = normalize(proj)
    img_emb = img_unit.astype(jnp.bfloat16)
    tea_img_emb = normalize(tea_img)[0].astype(jnp.bfloat16)
    txt_unit, txt_norm = normalize(stu_txt)
    txt_emb = txt_unit.astype(jnp.bfloat16)
    tea_txt_emb = normalize(tea_txt)[0].astype(jnp.bfloat16)
    block = math.gcd(pair_count, 512)
    blocks = pair_count // block
    txt_blocks = txt_emb.reshape(blocks, block, emb_width)
    tea_blocks = tea_txt_emb.reshape(blocks, block, tea_txt.shape[1])

    def advance(img_grads, pieces):
        txt_piece, tea_piece = pieces
        coef = affinity_tile(img_emb, tea_img_emb, txt_piece, tea_piece, factor)
        img_grads = img_grads + jnp.dot(coef, txt_piece, preferred_element_type=jnp.float32)
        text_part = lax.dot_general(coef, img_emb, (((0,), (0,)), ((), ())), preferred_element_type=jnp.float32)
        return (img_grads, text_part)
    img_grads, text_parts = lax.scan(advance, jnp.zeros((pair_count, emb_width), jnp.float32), (txt_blocks, tea_blocks))
    txt_grads = text_parts.reshape(pair_count, emb_width)
    grad_proj = ((img_grads - img_unit * lax.optimization_barrier(jnp.sum(img_unit * img_grads, axis=1, keepdims=True))) / proj_norm).astype(jnp.bfloat16)
    grad_head = lax.dot_general(images, grad_proj, (((0,), (0,)), ((), ())), preferred_element_type=jnp.float32)
    grad_images = lax.dot_general(grad_proj, head, (((1,), (1,)), ((), ())), preferred_element_type=jnp.float32)
    grad_text = (txt_grads - txt_unit * lax.optimization_barrier(jnp.sum(txt_unit * txt_grads, axis=1, keepdims=True))) / txt_norm
    return (grad_images, grad_head, grad_text)
```

```python
import functools
import jax
import jax.numpy as jnp
from jax import lax
from jax.experimental import pallas as pl
from jax.experimental.pallas import tpu as pltpu
from jax.sharding import PartitionSpec as P

logit_scale = 64.0
logit_bias = -2.0
loss_scale = 65536.0
half_scale = 0.5 * logit_scale
half_bias = 0.5 * logit_bias
bf16 = jnp.bfloat16
f32 = jnp.float32
NT = (((1,), (1,)), ((), ()))
TN = (((0,), (0,)), ((), ()))


def params():
    return pltpu.CompilerParams(vmem_limit_bytes=48 * 1024 * 1024)


def cost(flops, moved, trans=0):
    return pl.CostEstimate(flops=int(flops), bytes_accessed=int(moved), transcendentals=int(trans))


def swap(value, axis, mask):
    count = lax.axis_size(axis)
    return lax.ppermute(value, axis, [(source, source ^ mask) for source in range(count)])


def inverse_length(floats):
    return lax.rsqrt(jnp.sum(floats * floats, axis=1, keepdims=True) + 1e-06)


def text_kernel(tea_ref, stu_ref, low_ref, high_ref):
    half, tea_width = low_ref.shape[0], tea_ref.shape[1]
    for place, out_ref in enumerate((low_ref, high_ref)):
        rows = pl.ds(place * half, half)
        tea = tea_ref[rows, :].astype(f32)
        out_ref[:, :tea_width] = (tea * inverse_length(tea)).astype(bf16)
        stu = stu_ref[rows, :].astype(f32)
        out_ref[:, tea_width:] = (stu * inverse_length(stu)).astype(bf16)


def text_parts(tea_txt, stu_txt):
    share, tea_width = tea_txt.shape
    width = tea_width + stu_txt.shape[1]
    part = jax.ShapeDtypeStruct((share // 2, width), bf16)
    return pl.pallas_call(
        text_kernel,
        out_shape=(part, part),
        compiler_params=params(),
        cost_estimate=cost(4 * share * width, 4 * share * width),
    )(tea_txt, stu_txt)


def teacher_kernel(tea_ref, out_ref):
    tea = tea_ref[...].astype(f32)
    out_ref[...] = (tea * inverse_length(tea)).astype(bf16) * half_scale


def teacher_emb(tea_img, chunk):
    rows, width = tea_img.shape
    spec = pl.BlockSpec((chunk, width), lambda i: (i, 0))
    return pl.pallas_call(
        teacher_kernel,
        grid=(rows // chunk,),
        in_specs=[spec],
        out_specs=spec,
        out_shape=jax.ShapeDtypeStruct((rows, width), bf16),
        compiler_params=params(),
        cost_estimate=cost(4 * rows * width, 4 * rows * width),
    )(tea_img)


def proj_kernel(order_ref, images_ref, near_ref, far_ref, proj_ref, emb_ref, head_ref):
    columns = near_ref.shape[1]
    count = near_ref.shape[0]

    @pl.when(pl.program_id(0) == 0)
    def _():
        for k in range(count):
            for place, ref in enumerate((near_ref, far_ref)):
                start = pl.multiple_of(order_ref[2 * k + place] * columns, columns)
                head_ref[pl.ds(start, columns), :] = ref[k]

    proj = lax.dot_general(images_ref[...], head_ref[...], NT, preferred_element_type=f32).astype(bf16)
    floats = proj.astype(f32)
    proj_ref[...] = proj
    emb_ref[...] = (floats * inverse_length(floats)).astype(bf16) * half_scale


def projections(order, images, near, far, chunk):
    rows, depth = images.shape
    count, columns, _ = near.shape
    width = 2 * count * columns
    piece = pl.BlockSpec((count, columns, depth), lambda i, order: (0, 0, 0))
    row = pl.BlockSpec((chunk, width), lambda i, order: (i, 0))
    return pl.pallas_call(
        proj_kernel,
        grid_spec=pltpu.PrefetchScalarGridSpec(
            num_scalar_prefetch=1,
            grid=(rows // chunk,),
            in_specs=[pl.BlockSpec((chunk, depth), lambda i, order: (i, 0)), piece, piece],
            out_specs=[row, row, pl.BlockSpec((width, depth), lambda i, order: (0, 0))],
        ),
        out_shape=(
            jax.ShapeDtypeStruct((rows, width), bf16),
            jax.ShapeDtypeStruct((rows, width), bf16),
            jax.ShapeDtypeStruct((width, depth), bf16),
        ),
        compiler_params=params(),
        cost_estimate=cost(2 * rows * depth * width, 6 * rows * depth),
    )(order, images, near, far)


def pair_tile(tea_ref, emb_ref, texts, grads_ref):
    tea_width = tea_ref.shape[1]
    emb = emb_ref[...]
    target = lax.dot_general(tea_ref[...], texts[:, :tea_width], NT, preferred_element_type=f32)
    student = lax.dot_general(emb, texts[:, tea_width:], NT, preferred_element_type=f32)
    coef = (jnp.tanh(student + half_bias) - jnp.tanh(target + half_bias)).astype(bf16)
    grads_ref[...] += lax.dot_general(coef, emb, TN, preferred_element_type=f32)
    return jnp.dot(coef, texts[:, tea_width:], preferred_element_type=f32)


def early_kernel(count, summed, *refs):
    tea_ref, emb_ref = refs[:2]
    text_refs = refs[2 : 2 + count]
    refs = refs[2 + count :]
    if summed:
        before_ref, refs = refs[0], refs[1:]
    out_ref, grads_ref, texts_ref = refs
    half = text_refs[0].shape[0]

    @pl.when(pl.program_id(0) == 0)
    def _():
        for k in range(count):
            texts_ref[pl.ds(k * half, half), :] = text_refs[k][...]
        grads_ref[...] = jnp.zeros_like(grads_ref)

    grads = pair_tile(tea_ref, emb_ref, texts_ref, grads_ref)
    out_ref[...] = grads + before_ref[...] if summed else grads


def early(tea_emb, emb, texts, before, chunk):
    rows, tea_width = tea_emb.shape
    emb_width = emb.shape[1]
    half, width = texts[0].shape
    count = len(texts)
    size = count * half
    row = lambda wide: pl.BlockSpec((chunk, wide), lambda i: (i, 0))
    whole = lambda shape: pl.BlockSpec(shape, lambda i: (0, 0))
    given = [tea_emb, emb, *texts] + ([] if before is None else [before])
    return pl.pallas_call(
        functools.partial(early_kernel, count, before is not None),
        grid=(rows // chunk,),
        in_specs=[row(tea_width), row(emb_width)]
        + [whole((half, width))] * count
        + ([] if before is None else [row(emb_width)]),
        out_specs=[row(emb_width), whole((size, emb_width))],
        out_shape=(
            jax.ShapeDtypeStruct((rows, emb_width), f32),
            jax.ShapeDtypeStruct((size, emb_width), f32),
        ),
        scratch_shapes=[pltpu.VMEM((size, width), bf16)],
        compiler_params=params(),
        cost_estimate=cost(2 * rows * size * (width + 2 * emb_width), 2 * rows * (width + 4 * emb_width)),
    )(*given)


def late_kernel(count, masks, summed, order_ref, *refs):
    tea_ref, emb_ref, proj_ref, before_ref = refs[:4]
    text_refs = refs[4 : 4 + count]
    refs = refs[4 + count :]
    if summed:
        texts_before_ref, refs = refs[0], refs[1:]
    give_ref, keep_refs, grads_ref, texts_ref = refs[0], refs[1 : 1 + masks], refs[-2], refs[-1]
    half = text_refs[0].shape[0]
    share = tea_ref.shape[0]
    step = pl.program_id(0)

    @pl.when(step == 0)
    def _():
        for k in range(count):
            texts_ref[pl.ds(k * half, half), :] = text_refs[k][...]
        grads_ref[...] = texts_before_ref[...] if summed else jnp.zeros_like(grads_ref)

    grads = pair_tile(tea_ref, emb_ref, texts_ref, grads_ref) + before_ref[...]
    floats = proj_ref[...].astype(f32)
    inverse = inverse_length(floats)
    unit = floats * inverse
    along = jnp.sum(unit * grads, axis=1, keepdims=True)
    part = ((grads - unit * along) * inverse).astype(bf16)
    for k in range(masks):

        @pl.when(step == 2 * k)
        def _(k=k):
            give_ref[pl.ds(k * share, share), :] = part

        @pl.when(step == 2 * k + 1)
        def _(k=k):
            keep_refs[k][...] = part


def late(order, tea_emb, emb, proj, before, texts, texts_before, share):
    rows, tea_width = tea_emb.shape
    emb_width = emb.shape[1]
    half, width = texts[0].shape
    count = len(texts)
    size = count * half
    steps = order.shape[0]
    masks = steps // 2
    row = lambda wide: pl.BlockSpec((share, wide), lambda i, order: (order[i], 0))
    whole = lambda shape: pl.BlockSpec(shape, lambda i, order: (0, 0))
    summed = texts_before is not None
    given = [tea_emb, emb, proj, before, *texts] + ([texts_before] if summed else [])
    out = pl.pallas_call(
        functools.partial(late_kernel, count, masks, summed),
        grid_spec=pltpu.PrefetchScalarGridSpec(
            num_scalar_prefetch=1,
            grid=(steps,),
            in_specs=[row(tea_width), row(emb_width), row(emb_width), row(emb_width)]
            + [whole((half, width))] * count
            + ([whole((size, emb_width))] if summed else []),
            out_specs=[whole((masks * share, emb_width))]
            + [whole((share, emb_width))] * masks
            + [whole((size, emb_width))],
            scratch_shapes=[pltpu.VMEM((size, width), bf16)],
        ),
        out_shape=[jax.ShapeDtypeStruct((masks * share, emb_width), bf16)]
        + [jax.ShapeDtypeStruct((share, emb_width), bf16)] * masks
        + [jax.ShapeDtypeStruct((size, emb_width), f32)],
        compiler_params=params(),
        cost_estimate=cost(
            2 * steps * share * size * (width + 2 * emb_width), 2 * steps * share * (width + 4 * emb_width)
        ),
    )(order, *given)
    return out[0], out[1:-1], out[-1]


def head_kernel(count, order_ref, images_ref, *refs):
    part_refs = refs[:count]
    near_ref, far_ref, total_ref = refs[count:]
    columns = near_ref.shape[0] // count
    step = pl.program_id(0)

    @pl.when(step == 0)
    def _():
        total_ref[...] = jnp.zeros_like(total_ref)

    for k in range(count):

        @pl.when(step == k)
        def _(k=k):
            total_ref[...] += lax.dot_general(
                part_refs[k][...], images_ref[...], TN, preferred_element_type=f32
            )

    @pl.when(step == count - 1)
    def _():
        for k in range(count):
            for place, ref in enumerate((near_ref, far_ref)):
                start = pl.multiple_of(order_ref[2 * k + place] * columns, columns)
                ref[pl.ds(k * columns, columns), :] = total_ref[pl.ds(start, columns), :].astype(bf16)


def head_parts(order, images, parts, columns):
    depth = images.shape[1]
    share, width = parts[0].shape
    count = len(parts)
    whole = lambda shape: pl.BlockSpec(shape, lambda i, order: (0, 0))
    piece = jax.ShapeDtypeStruct((count * columns, depth), bf16)
    return pl.pallas_call(
        functools.partial(head_kernel, count),
        grid_spec=pltpu.PrefetchScalarGridSpec(
            num_scalar_prefetch=1,
            grid=(count,),
            in_specs=[pl.BlockSpec((share, depth), lambda i, order: (order[2 * i], 0))]
            + [whole((share, width))] * count,
            out_specs=[whole(piece.shape)] * 2,
            scratch_shapes=[pltpu.VMEM((width, depth), f32)],
        ),
        out_shape=(piece, piece),
        compiler_params=params(),
        cost_estimate=cost(2 * count * share * width * depth, 4 * count * share * width),
    )(order, images, *parts)


def images_kernel(scale, *refs):
    part_refs, head_ref, out_ref = refs[:-2], refs[-2], refs[-1]
    total = part_refs[0][...].astype(f32)
    for ref in part_refs[1:]:
        total += ref[...].astype(f32)
    out_ref[...] = scale * jnp.dot(total.astype(bf16), head_ref[...], preferred_element_type=f32)


def image_grads(parts, head, scale):
    share, width = parts[0].shape
    depth = head.shape[1]
    return pl.pallas_call(
        functools.partial(images_kernel, scale),
        out_shape=jax.ShapeDtypeStruct((share, depth), f32),
        compiler_params=params(),
        cost_estimate=cost(2 * share * width * depth, 4 * share * width),
    )(*parts, head)


def per_device(images, head, tea_img, stu_txt, tea_txt):
    dp_count = lax.axis_size("dp")
    tensor_count = lax.axis_size("tensor")
    rank = lax.axis_index("tensor")
    rows = images.shape[0]
    columns = head.shape[1]
    share = rows // tensor_count
    half = share // 2
    pairs = tensor_count // 2
    bits = dp_count.bit_length() - 1
    chunk = 2 * share
    factor = 0.5 * logit_scale * loss_scale / (rows * dp_count)

    low, high = text_parts(tea_txt, stu_txt)
    lows, highs = {0: low}, {0: high}
    for stage in range(bits):
        for mask in list(lows):
            lows[mask ^ (1 << stage)] = swap(lows[mask], "dp", 1 << stage)
        for mask in list(highs):
            other = 1 << (bits - 1 - stage)
            highs[mask ^ other] = swap(highs[mask], "dp", other)

    head_t = head.T
    near = jnp.stack([head_t] + [swap(head_t, "tensor", 2 * k) for k in range(1, pairs)])
    far = swap(near, "tensor", 1)
    order = jnp.stack([rank ^ (2 * k + place) for k in range(pairs) for place in range(2)]).astype(jnp.int32)

    tea_emb = teacher_emb(tea_img, chunk)
    proj, emb, head_full = projections(order, images, near, far, chunk)

    text_grads = {}
    image_part, text_grads[0] = early(tea_emb, emb, [lows[0], highs[0]], None, chunk)
    middle = list(range(1, dp_count - 1))
    texts = [part for mask in middle for part in (lows[mask], highs[mask])]
    image_part, grads = early(tea_emb, emb, texts, image_part, chunk)
    for k, mask in enumerate(middle):
        text_grads[mask] = grads[k * share : (k + 1) * share]
    last = dp_count - 1
    first_masks = list(range(pairs // 2, pairs))[::-1]
    second_masks = list(range(pairs // 2))[::-1]
    orders = [
        jnp.stack([rank ^ (2 * k + place) for k in masks for place in (1, 0)]).astype(jnp.int32)
        for masks in (first_masks, second_masks)
    ]
    texts = [lows[last], highs[last]]
    give_a, keep_a, grads = late(orders[0], tea_emb, emb, proj, image_part, texts, None, share)
    take_a = swap(give_a, "tensor", 1)
    give_b, keep_b, grads = late(orders[1], tea_emb, emb, proj, image_part, texts, grads, share)
    take_b = swap(give_b, "tensor", 1)
    text_grads[last] = grads

    reduced = {}
    for masks, keep, take in ((first_masks, keep_a, take_a), (second_masks, keep_b, take_b)):
        for k, mask in enumerate(masks):
            reduced[mask] = keep[k] + take[k * share : (k + 1) * share]
    arrived = [swap(reduced[mask], "tensor", 2 * mask) for mask in range(1, pairs)[::-1]]
    grad_images = image_grads([reduced[0]] + arrived, head_full, factor)

    sums = []
    for part in range(2):
        held = {m: text_grads[m][part * half : (part + 1) * half] for m in range(dp_count)}
        for stage in range(bits):
            bit = 1 << ((bits - 1 - stage) if part == 0 else stage)
            sent = [m for m in sorted(held) if m & bit]
            got = swap(jnp.stack([held[m] for m in sent]).astype(bf16), "dp", bit)
            for k, m in enumerate(sent):
                held[m ^ bit] = held[m ^ bit] + got[k].astype(f32)
                del held[m]
        sums.append(held[0])
    total = jnp.concatenate(sums) * (factor / half_scale)
    stu = stu_txt.astype(f32)
    inverse = inverse_length(stu)
    unit = stu * inverse
    grad_text = (total - unit * jnp.sum(unit * total, axis=1, keepdims=True)) * inverse

    near_part, far_part = head_parts(order, images, [reduced[mask] for mask in range(pairs)], columns)
    summed = near_part + swap(far_part, "tensor", 1)
    pieces = summed.reshape(pairs, columns, images.shape[1])
    own = pieces[0].astype(f32)
    for k in range(1, pairs):
        own = own + swap(pieces[k], "tensor", 2 * k).astype(f32)
    for bit in range(bits):
        rounded = lax.reduce_precision(own, 8, 7)
        own = rounded + swap(rounded.astype(bf16), "dp", 1 << bit).astype(f32)
    grad_head = own.T * factor
    return (grad_images, grad_head, grad_text)


def solution(mesh):
    placed = (
        P("dp", None),
        P(None, "tensor"),
        P("dp", None),
        P(("dp", "tensor"), None),
        P(("dp", "tensor"), None),
    )
    return jax.shard_map(
        per_device,
        mesh=mesh,
        in_specs=placed,
        out_specs=(P(("dp", "tensor"), None), P(None, "tensor"), P(("dp", "tensor"), None)),
        check_vma=False,
    )
```

```python
import functools
import math
import jax
import jax.numpy as jnp
from jax import lax
from jax.experimental import pallas as pl
from jax.experimental.pallas import tpu as pltpu
from jax.sharding import PartitionSpec as P

logit_scale = 64.0
logit_bias = -2.0
loss_scale = 65536.0
half_scale = 0.5 * logit_scale
half_bias = 0.5 * logit_bias
bf16 = jnp.bfloat16
f32 = jnp.float32
NT = (((1,), (1,)), ((), ()))
TN = (((0,), (0,)), ((), ()))


def params():
    return pltpu.CompilerParams(vmem_limit_bytes=22 * 1024 * 1024)


resident = pl.BlockSpec(memory_space=pltpu.VMEM)


def pinned(value):
    return pltpu.with_memory_space_constraint(value, pltpu.VMEM)


def cost(flops, moved, trans=0):
    return pl.CostEstimate(flops=int(flops), bytes_accessed=int(moved), transcendentals=int(trans))


def swap(value, axis, mask):
    count = lax.axis_size(axis)
    return lax.ppermute(value, axis, [(source, source ^ mask) for source in range(count)])


def inverse_length(floats):
    return lax.rsqrt(jnp.sum(floats * floats, axis=1, keepdims=True) + 1e-06)


def text_kernel(tea_ref, stu_ref, low_ref, high_ref):
    half, tea_width = low_ref.shape[0], tea_ref.shape[1]
    for place, out_ref in enumerate((low_ref, high_ref)):
        rows = pl.ds(place * half, half)
        tea = tea_ref[rows, :].astype(f32)
        out_ref[:, :tea_width] = (tea * inverse_length(tea)).astype(bf16)
        stu = stu_ref[rows, :].astype(f32)
        out_ref[:, tea_width:] = (stu * inverse_length(stu)).astype(bf16)


def text_parts(tea_txt, stu_txt):
    share, tea_width = tea_txt.shape
    width = tea_width + stu_txt.shape[1]
    part = jax.ShapeDtypeStruct((share // 2, width), bf16)
    return pl.pallas_call(
        text_kernel,
        out_shape=(part, part),
        compiler_params=params(),
        cost_estimate=cost(4 * share * width, 4 * share * width),
    )(tea_txt, stu_txt)


def teacher_kernel(tea_ref, out_ref):
    chunk = tea_ref.shape[0]
    rows = pl.ds(pl.multiple_of(pl.program_id(0) * chunk, chunk), chunk)
    tea = tea_ref[...].astype(f32)
    out_ref[rows, :] = (tea * inverse_length(tea)).astype(bf16) * half_scale


def teacher_emb(tea_img):
    rows, width = tea_img.shape
    chunk = math.gcd(rows, 512)
    return pl.pallas_call(
        teacher_kernel,
        grid=(rows // chunk,),
        in_specs=[pl.BlockSpec((chunk, width), lambda i: (i, 0))],
        out_specs=resident,
        out_shape=pltpu.VMEM((rows, width), bf16),
        compiler_params=params(),
        cost_estimate=cost(4 * rows * width, 2 * rows * width),
    )(tea_img)


def proj_kernel(order_ref, images_ref, near_ref, far_ref, proj_ref, emb_ref, head_ref):
    count, columns = near_ref.shape[:2]
    chunk = images_ref.shape[0]

    @pl.when(pl.program_id(0) == 0)
    def _():
        for k in range(count):
            for place, ref in enumerate((near_ref, far_ref)):
                start = pl.multiple_of(order_ref[2 * k + place] * columns, columns)
                head_ref[pl.ds(start, columns), :] = ref[k]

    rows = pl.ds(pl.multiple_of(pl.program_id(0) * chunk, chunk), chunk)
    proj = lax.dot_general(images_ref[...], head_ref[...], NT, preferred_element_type=f32).astype(bf16)
    floats = proj.astype(f32)
    proj_ref[rows, :] = proj
    emb_ref[rows, :] = (floats * inverse_length(floats)).astype(bf16) * half_scale


def projections(order, images, near, far):
    rows, depth = images.shape
    count, columns, _ = near.shape
    width = 2 * count * columns
    chunk = math.gcd(rows, 512)
    return pl.pallas_call(
        proj_kernel,
        grid_spec=pltpu.PrefetchScalarGridSpec(
            num_scalar_prefetch=1,
            grid=(rows // chunk,),
            in_specs=[pl.BlockSpec((chunk, depth), lambda i, order: (i, 0)), resident, resident],
            out_specs=[resident, resident, resident],
        ),
        out_shape=(
            pltpu.VMEM((rows, width), bf16),
            pltpu.VMEM((rows, width), bf16),
            jax.ShapeDtypeStruct((width, depth), bf16),
        ),
        compiler_params=params(),
        cost_estimate=cost(2 * rows * depth * width, 2 * rows * depth),
    )(order, images, near, far)


def pair_tile(tea, emb, texts, grads_ref):
    tea_width = tea.shape[1]
    target = lax.dot_general(tea, texts[:, :tea_width], NT, preferred_element_type=f32)
    student = lax.dot_general(emb, texts[:, tea_width:], NT, preferred_element_type=f32)
    coef = (jnp.tanh(student + half_bias) - jnp.tanh(target + half_bias)).astype(bf16)
    part = jnp.dot(coef, texts[:, tea_width:], preferred_element_type=f32)
    grads_ref[...] += lax.dot_general(coef, emb, TN, preferred_element_type=f32)
    return part


def early_kernel(count, summed, *refs):
    tea_ref, emb_ref = refs[:2]
    text_refs = refs[2 : 2 + count]
    refs = refs[2 + count :]
    if summed:
        before_ref, refs = refs[0], refs[1:]
    out_ref, grads_ref, texts_ref = refs
    half = text_refs[0].shape[0]
    size = tea_ref.shape[0]
    chunk = math.gcd(size, 512)
    for k in range(count):
        texts_ref[pl.ds(k * half, half), :] = text_refs[k][...]
    grads_ref[...] = jnp.zeros_like(grads_ref)
    for k in range(size // chunk):
        rows = pl.ds(k * chunk, chunk)
        part = pair_tile(tea_ref[rows, :], emb_ref[rows, :], texts_ref, grads_ref)
        out_ref[rows, :] = part + before_ref[rows, :] if summed else part


def early(tea_emb, emb, texts, before):
    rows = tea_emb.shape[0]
    emb_width = emb.shape[1]
    half, width = texts[0].shape
    count = len(texts)
    size = count * half
    given = [pinned(tea_emb), pinned(emb), *texts] + ([] if before is None else [pinned(before)])
    return pl.pallas_call(
        functools.partial(early_kernel, count, before is not None),
        in_specs=[resident] * len(given),
        out_specs=[resident, resident],
        out_shape=(
            pltpu.VMEM((rows, emb_width), f32),
            jax.ShapeDtypeStruct((size, emb_width), f32),
        ),
        input_output_aliases={} if before is None else {len(given) - 1: 0},
        scratch_shapes=[pltpu.VMEM((size, width), bf16)],
        compiler_params=params(),
        cost_estimate=cost(2 * rows * size * (width + 2 * emb_width), 2 * size * (width + 2 * emb_width)),
    )(*given)


def late_kernel(count, masks, summed, order_ref, *refs):
    tea_ref, emb_ref, proj_ref, before_ref = refs[:4]
    text_refs = refs[4 : 4 + count]
    refs = refs[4 + count :]
    if summed:
        texts_before_ref, refs = refs[0], refs[1:]
    give_ref, keep_refs, grads_ref, texts_ref, part_ref = refs[0], refs[1 : 1 + masks], *refs[-3:]
    half = text_refs[0].shape[0]
    share = keep_refs[0].shape[0]
    for k in range(count):
        texts_ref[pl.ds(k * half, half), :] = text_refs[k][...]
    grads_ref[...] = texts_before_ref[...] if summed else jnp.zeros_like(grads_ref)
    for k in range(masks):
        rows = pl.ds(pl.multiple_of(order_ref[k] * (2 * share), 2 * share), 2 * share)
        grads = pair_tile(tea_ref[rows, :], emb_ref[rows, :], texts_ref, grads_ref) + before_ref[rows, :]
        floats = proj_ref[rows, :].astype(f32)
        inverse = inverse_length(floats)
        unit = floats * inverse
        along = jnp.sum(unit * grads, axis=1, keepdims=True)
        part_ref[...] = ((grads - unit * along) * inverse).astype(bf16)
        side = order_ref[masks]
        keep_refs[k][...] = part_ref[pl.ds(pl.multiple_of(side * share, share), share), :]
        give_ref[pl.ds(k * share, share), :] = part_ref[pl.ds(pl.multiple_of((1 - side) * share, share), share), :]


def late(order, tea_emb, emb, proj, before, texts, texts_before, share):
    tea_width, emb_width = tea_emb.shape[1], emb.shape[1]
    half, width = texts[0].shape
    count = len(texts)
    size = count * half
    masks = order.shape[0] - 1
    summed = texts_before is not None
    given = [pinned(tea_emb), pinned(emb), pinned(proj), pinned(before), *texts]
    given += [texts_before] if summed else []
    out = pl.pallas_call(
        functools.partial(late_kernel, count, masks, summed),
        in_specs=[pl.BlockSpec(memory_space=pltpu.SMEM)] + [resident] * len(given),
        out_specs=[resident] * (masks + 2),
        out_shape=[jax.ShapeDtypeStruct((masks * share, emb_width), bf16)]
        + [jax.ShapeDtypeStruct((share, emb_width), bf16)] * masks
        + [jax.ShapeDtypeStruct((size, emb_width), f32)],
        scratch_shapes=[pltpu.VMEM((size, width), bf16), pltpu.VMEM((2 * share, emb_width), bf16)],
        compiler_params=params(),
        cost_estimate=cost(
            4 * masks * share * size * (width + 2 * emb_width), 4 * masks * share * emb_width
        ),
    )(order, *given)
    return out[0], out[1:-1], out[-1]


def head_kernel(count, order_ref, images_ref, *refs):
    part_refs = refs[:count]
    near_ref, far_ref, total_ref = refs[count:]
    columns = near_ref.shape[0] // count
    step = pl.program_id(0)

    @pl.when(step == 0)
    def _():
        total_ref[...] = jnp.zeros_like(total_ref)

    for k in range(count):

        @pl.when(step == k)
        def _(k=k):
            total_ref[...] += lax.dot_general(
                part_refs[k][...], images_ref[...], TN, preferred_element_type=f32
            )

    @pl.when(step == count - 1)
    def _():
        for k in range(count):
            for place, ref in enumerate((near_ref, far_ref)):
                start = pl.multiple_of(order_ref[2 * k + place] * columns, columns)
                ref[pl.ds(k * columns, columns), :] = total_ref[pl.ds(start, columns), :].astype(bf16)


def head_parts(order, images, parts, columns):
    depth = images.shape[1]
    share, width = parts[0].shape
    count = len(parts)
    whole = lambda shape: pl.BlockSpec(shape, lambda i, order: (0, 0))
    piece = jax.ShapeDtypeStruct((count * columns, depth), bf16)
    return pl.pallas_call(
        functools.partial(head_kernel, count),
        grid_spec=pltpu.PrefetchScalarGridSpec(
            num_scalar_prefetch=1,
            grid=(count,),
            in_specs=[pl.BlockSpec((share, depth), lambda i, order: (order[2 * i], 0))]
            + [whole((share, width))] * count,
            out_specs=[whole(piece.shape)] * 2,
            scratch_shapes=[pltpu.VMEM((width, depth), f32)],
        ),
        out_shape=(piece, piece),
        compiler_params=params(),
        cost_estimate=cost(2 * count * share * width * depth, 4 * count * share * width),
    )(order, images, *parts)


def images_kernel(scale, *refs):
    part_refs, head_ref, out_ref = refs[:-2], refs[-2], refs[-1]
    total = part_refs[0][...].astype(f32)
    for ref in part_refs[1:]:
        total += ref[...].astype(f32)
    out_ref[...] = scale * jnp.dot(total.astype(bf16), head_ref[...], preferred_element_type=f32)


def image_grads(parts, head, scale):
    share, width = parts[0].shape
    depth = head.shape[1]
    return pl.pallas_call(
        functools.partial(images_kernel, scale),
        out_shape=jax.ShapeDtypeStruct((share, depth), f32),
        compiler_params=params(),
        cost_estimate=cost(2 * share * width * depth, 4 * share * width),
    )(*parts, head)


def per_device(images, head, tea_img, stu_txt, tea_txt):
    dp_count = lax.axis_size("dp")
    tensor_count = lax.axis_size("tensor")
    rank = lax.axis_index("tensor")
    rows = images.shape[0]
    columns = head.shape[1]
    share = rows // tensor_count
    half = share // 2
    pairs = tensor_count // 2
    bits = dp_count.bit_length() - 1
    factor = 0.5 * logit_scale * loss_scale / (rows * dp_count)

    low, high = text_parts(tea_txt, stu_txt)
    lows, highs = {0: low}, {0: high}
    for stage in range(bits):
        for mask in list(lows):
            lows[mask ^ (1 << stage)] = swap(lows[mask], "dp", 1 << stage)
        for mask in list(highs):
            other = 1 << (bits - 1 - stage)
            highs[mask ^ other] = swap(highs[mask], "dp", other)

    head_t = head.T
    near = jnp.stack([head_t] + [swap(head_t, "tensor", 2 * k) for k in range(1, pairs)])
    far = swap(near, "tensor", 1)
    order = jnp.stack([rank ^ (2 * k + place) for k in range(pairs) for place in range(2)]).astype(jnp.int32)

    tea_emb = teacher_emb(tea_img)
    proj, emb, head_full = projections(order, images, near, far)

    text_grads = {}
    image_part, text_grads[0] = early(tea_emb, emb, [lows[0], highs[0]], None)
    middle = list(range(1, dp_count - 1))
    texts = [part for mask in middle for part in (lows[mask], highs[mask])]
    image_part, grads = early(tea_emb, emb, texts, image_part)
    for k, mask in enumerate(middle):
        text_grads[mask] = grads[k * share : (k + 1) * share]
    last = dp_count - 1
    first_masks = list(range(pairs // 2, pairs))[::-1]
    second_masks = list(range(pairs // 2))[::-1]
    orders = [
        jnp.stack([(rank // 2) ^ k for k in masks] + [rank % 2]).astype(jnp.int32)
        for masks in (first_masks, second_masks)
    ]
    texts = [lows[last], highs[last]]
    give_a, keep_a, grads = late(orders[0], tea_emb, emb, proj, image_part, texts, None, share)
    take_a = swap(give_a, "tensor", 1)
    give_b, keep_b, grads = late(orders[1], tea_emb, emb, proj, image_part, texts, grads, share)
    take_b = swap(give_b, "tensor", 1)
    text_grads[last] = grads

    reduced = {}
    for masks, keep, take in ((first_masks, keep_a, take_a), (second_masks, keep_b, take_b)):
        for k, mask in enumerate(masks):
            reduced[mask] = keep[k] + take[k * share : (k + 1) * share]
    arrived = [swap(reduced[mask], "tensor", 2 * mask) for mask in range(1, pairs)[::-1]]
    grad_images = image_grads([reduced[0]] + arrived, head_full, factor)

    sums = []
    for part in range(2):
        held = {m: text_grads[m][part * half : (part + 1) * half] for m in range(dp_count)}
        for stage in range(bits):
            bit = 1 << ((bits - 1 - stage) if part == 0 else stage)
            sent = [m for m in sorted(held) if m & bit]
            got = swap(jnp.stack([held[m] for m in sent]).astype(bf16), "dp", bit)
            for k, m in enumerate(sent):
                held[m ^ bit] = held[m ^ bit] + got[k].astype(f32)
                del held[m]
        sums.append(held[0])
    total = jnp.concatenate(sums) * (factor / half_scale)
    stu = stu_txt.astype(f32)
    inverse = inverse_length(stu)
    unit = stu * inverse
    grad_text = (total - unit * jnp.sum(unit * total, axis=1, keepdims=True)) * inverse

    near_part, far_part = head_parts(order, images, [reduced[mask] for mask in range(pairs)], columns)
    summed = near_part + swap(far_part, "tensor", 1)
    pieces = summed.reshape(pairs, columns, images.shape[1])
    own = pieces[0].astype(f32)
    for k in range(1, pairs):
        own = own + swap(pieces[k], "tensor", 2 * k).astype(f32)
    for bit in range(bits):
        rounded = lax.reduce_precision(own, 8, 7)
        own = rounded + swap(rounded.astype(bf16), "dp", 1 << bit).astype(f32)
    grad_head = own.T * factor
    return (grad_images, grad_head, grad_text)


def solution(mesh):
    placed = (
        P("dp", None),
        P(None, "tensor"),
        P("dp", None),
        P(("dp", "tensor"), None),
        P(("dp", "tensor"), None),
    )
    return jax.shard_map(
        per_device,
        mesh=mesh,
        in_specs=placed,
        out_specs=(P(("dp", "tensor"), None), P(None, "tensor"), P(("dp", "tensor"), None)),
        check_vma=False,
    )
```

```python
import functools
import math
import jax
import jax.numpy as jnp
from jax import lax
from jax.experimental import pallas as pl
from jax.experimental.pallas import tpu as pltpu
from jax.sharding import PartitionSpec as P

logit_scale = 64.0
logit_bias = -2.0
loss_scale = 65536.0
half_scale = 0.5 * logit_scale
half_bias = 0.5 * logit_bias
bf16 = jnp.bfloat16
f32 = jnp.float32
NT = (((1,), (1,)), ((), ()))
TN = (((0,), (0,)), ((), ()))


def params(held=0):
    return pltpu.CompilerParams(vmem_limit_bytes=held + 10 * 1024 * 1024)


resident = pl.BlockSpec(memory_space=pltpu.VMEM)


def pinned(value):
    return pltpu.with_memory_space_constraint(value, pltpu.VMEM)


def cost(flops, moved, trans=0):
    return pl.CostEstimate(flops=int(flops), bytes_accessed=int(moved), transcendentals=int(trans))


def swap(value, axis, mask):
    count = lax.axis_size(axis)
    return lax.ppermute(value, axis, [(source, source ^ mask) for source in range(count)])


def inverse_length(floats):
    return lax.rsqrt(jnp.sum(floats * floats, axis=1, keepdims=True) + 1e-06)


def in_hbm(value):
    return pltpu.with_memory_space_constraint(value, pltpu.HBM)


def stack_kernel(*refs):
    piece_refs, out_ref = refs[:-1], refs[-1]
    for k, ref in enumerate(piece_refs):
        out_ref[k, :, :] = ref[...]


def stacked(pieces):
    shape = (len(pieces), *pieces[0].shape)
    return pl.pallas_call(
        stack_kernel,
        in_specs=[resident] * len(pieces),
        out_specs=resident,
        out_shape=jax.ShapeDtypeStruct(shape, pieces[0].dtype),
        compiler_params=params(),
        cost_estimate=cost(0, 4 * math.prod(shape)),
    )(*pieces)


def sum_kernel(groups, *refs):
    start = 0
    for terms, out_ref in zip(groups, refs[-len(groups) :]):
        total = refs[start][...].astype(f32)
        for ref in refs[start + 1 : start + terms]:
            total += ref[...].astype(f32)
        out_ref[...] = total.astype(bf16)
        start += terms


def sums(groups, gates):
    given = [term for group in groups for term in group]
    size = sum(math.prod(term.shape) for term in given)
    return pl.pallas_call(
        functools.partial(sum_kernel, [len(group) for group in groups]),
        in_specs=[resident] * len(given) + [pl.BlockSpec(memory_space=pl.ANY)] * len(gates),
        out_specs=[resident] * len(groups),
        out_shape=[jax.ShapeDtypeStruct(group[0].shape, bf16) for group in groups],
        compiler_params=params(),
        cost_estimate=cost(0, 0),
    )(*given, *gates)


def fold_kernel(*refs):
    terms, (low_ref, high_ref) = refs[:-2], refs[-2:]
    half = low_ref.shape[0]
    for k, out_ref in enumerate((low_ref, high_ref)):
        total = terms[0][k * half : (k + 1) * half].astype(f32)
        for ref in terms[1:]:
            total += ref[k * half : (k + 1) * half].astype(f32)
        out_ref[...] = total.astype(bf16)


def folded(terms):
    count, *rest = terms[0].shape
    size = len(terms) * math.prod(terms[0].shape)
    return pl.pallas_call(
        fold_kernel,
        in_specs=[resident] * len(terms),
        out_specs=[resident] * 2,
        out_shape=[jax.ShapeDtypeStruct((count // 2, *rest), bf16)] * 2,
        compiler_params=params(),
        cost_estimate=cost(0, 0),
    )(*terms)


def text_kernel(tea_ref, stu_ref, low_ref, high_ref):
    tea_width = tea_ref.shape[1]
    for place, out_ref in enumerate((low_ref, high_ref)):

        @pl.when(pl.program_id(0) == place)
        def _(out_ref=out_ref):
            tea = tea_ref[...].astype(f32)
            out_ref[:, :tea_width] = (tea * inverse_length(tea)).astype(bf16)
            stu = stu_ref[...].astype(f32)
            out_ref[:, tea_width:] = (stu * inverse_length(stu)).astype(bf16)


def text_halves(tea_txt, stu_txt):
    share, tea_width = tea_txt.shape
    stu_width = stu_txt.shape[1]
    half = share // 2
    part = jax.ShapeDtypeStruct((half, tea_width + stu_width), bf16)
    row = lambda width: pl.BlockSpec((half, width), lambda i: (i, 0))
    return pl.pallas_call(
        text_kernel,
        grid=(2,),
        in_specs=[row(tea_width), row(stu_width)],
        out_specs=[resident] * 2,
        out_shape=(part, part),
        compiler_params=params(),
        cost_estimate=cost(4 * share * tea_width, 4 * share * tea_width),
    )(in_hbm(tea_txt), in_hbm(stu_txt))


def teacher_kernel(tea_ref, images_ref, low_ref, high_ref, emb_ref, target_ref, held_ref):
    chunk, width = tea_ref.shape
    rows = pl.ds(pl.multiple_of(pl.program_id(0) * chunk, chunk), chunk)
    tea = tea_ref[...].astype(f32)
    emb = (tea * inverse_length(tea)).astype(bf16) * half_scale
    emb_ref[rows, :] = emb
    half = low_ref.shape[0]
    for place, ref in enumerate((low_ref, high_ref)):
        target = lax.dot_general(emb, ref[:, :width], NT, preferred_element_type=f32)
        target_ref[rows, pl.ds(place * half, half)] = jnp.tanh(target + half_bias)
    held_ref[rows, :] = images_ref[...]


def teacher_emb(tea_img, images, low, high):
    rows, width = tea_img.shape
    depth = images.shape[1]
    chunk = math.gcd(rows, 512)
    size = 2 * low.shape[0]
    row = lambda width: pl.BlockSpec((chunk, width), lambda i: (i, 0))
    return pl.pallas_call(
        teacher_kernel,
        grid=(rows // chunk,),
        in_specs=[row(width), row(depth), resident, resident],
        out_specs=[resident] * 3,
        out_shape=(
            pltpu.VMEM((rows, width), bf16),
            pltpu.VMEM((rows, size), f32),
            pltpu.VMEM((rows, depth), bf16),
        ),
        compiler_params=params(),
        cost_estimate=cost(2 * rows * width * size, 2 * rows * width),
    )(in_hbm(tea_img), in_hbm(images), low, high)


def proj_kernel(order_ref, images_ref, near_ref, far_ref, _tea_ref, _target_ref, proj_ref, emb_ref, head_ref):
    count, columns = near_ref.shape[:2]
    size = images_ref.shape[0]
    chunk = math.gcd(size, 512)
    for k in range(count):
        for place, ref in enumerate((near_ref, far_ref)):
            start = pl.multiple_of(order_ref[2 * k + place] * columns, columns)
            head_ref[pl.ds(start, columns), :] = ref[k]
    for k in range(size // chunk):
        rows = pl.ds(k * chunk, chunk)
        proj = lax.dot_general(images_ref[rows, :], head_ref[...], NT, preferred_element_type=f32).astype(bf16)
        floats = proj.astype(f32)
        proj_ref[rows, :] = proj
        emb_ref[rows, :] = (floats * inverse_length(floats)).astype(bf16) * half_scale


def projections(order, images, near, far, *held):
    rows, depth = images.shape
    count, columns, _ = near.shape
    width = 2 * count * columns
    return pl.pallas_call(
        proj_kernel,
        in_specs=[pl.BlockSpec(memory_space=pltpu.SMEM)] + [resident] * (3 + len(held)),
        out_specs=[resident, resident, resident],
        out_shape=(
            pltpu.VMEM((rows, width), bf16),
            pltpu.VMEM((rows, width), bf16),
            jax.ShapeDtypeStruct((width, depth), bf16),
        ),
        compiler_params=params(),
        cost_estimate=cost(2 * rows * depth * width, 2 * rows * depth),
    )(order, pinned(images), near, far, *map(pinned, held))


def pair_tile(tea, emb, texts, grads_ref, target=None):
    stu = texts[:, -emb.shape[1] :]
    if target is None:
        target = lax.dot_general(tea, texts[:, : tea.shape[1]], NT, preferred_element_type=f32)
        target = jnp.tanh(target + half_bias)
    student = lax.dot_general(emb, stu, NT, preferred_element_type=f32)
    coef = (jnp.tanh(student + half_bias) - target).astype(bf16)
    part = jnp.dot(coef, stu, preferred_element_type=f32)
    grads_ref[...] += lax.dot_general(coef, emb, TN, preferred_element_type=f32)
    return part


def own_kernel(target_ref, emb_ref, low_ref, high_ref, _tea_ref, out_ref, grads_ref, texts_ref):
    width = emb_ref.shape[1]
    half = low_ref.shape[0]
    texts_ref[pl.ds(0, half), :] = low_ref[:, -width:]
    texts_ref[pl.ds(half, half), :] = high_ref[:, -width:]
    size = emb_ref.shape[0]
    chunk = math.gcd(size, 512)
    grads_ref[...] = jnp.zeros_like(grads_ref)
    for k in range(size // chunk):
        rows = pl.ds(k * chunk, chunk)
        out_ref[rows, :] = pair_tile(None, emb_ref[rows, :], texts_ref, grads_ref, target_ref[rows, :])


def own_texts(target, emb, low, high, tea_emb):
    rows, width = emb.shape
    size = target.shape[1]
    return pl.pallas_call(
        own_kernel,
        in_specs=[resident] * 5,
        out_specs=[resident, resident],
        out_shape=(pltpu.VMEM((rows, width), f32), jax.ShapeDtypeStruct((size, width), f32)),
        scratch_shapes=[pltpu.VMEM((size, width), bf16)],
        compiler_params=params(),
        cost_estimate=cost(6 * rows * size * width, 6 * size * width),
    )(pinned(target), pinned(emb), low, high, pinned(tea_emb))


def join(text_refs, out_ref):
    start = 0
    for ref in text_refs:
        out_ref[pl.ds(start, ref.shape[0]), :] = ref[...]
        start += ref.shape[0]


def early_kernel(count, *refs):
    tea_ref, emb_ref = refs[:2]
    text_refs = refs[2 : 2 + count]
    before_ref, out_ref, *sum_refs, grads_ref, texts_ref = refs[2 + count :]
    size = tea_ref.shape[0]
    chunk = math.gcd(size, 512)
    join(text_refs, texts_ref)
    grads_ref[...] = jnp.zeros_like(grads_ref)
    for k in range(size // chunk):
        rows = pl.ds(k * chunk, chunk)
        part = pair_tile(tea_ref[rows, :], emb_ref[rows, :], texts_ref, grads_ref)
        out_ref[rows, :] = part + before_ref[rows, :]
    share = grads_ref.shape[0] // len(sum_refs)
    for k, ref in enumerate(sum_refs):
        ref[...] = grads_ref[pl.ds(k * share, share), :].astype(bf16)


def early(tea_emb, emb, texts, before, share):
    rows = tea_emb.shape[0]
    emb_width = emb.shape[1]
    width = texts[0].shape[1]
    count = len(texts)
    size = sum(part.shape[0] for part in texts)
    given = [pinned(tea_emb), pinned(emb), *texts, pinned(before)]
    return pl.pallas_call(
        functools.partial(early_kernel, count),
        in_specs=[resident] * len(given),
        out_specs=[resident] * (1 + size // share),
        out_shape=[pltpu.VMEM((rows, emb_width), f32)]
        + [jax.ShapeDtypeStruct((share, emb_width), bf16)] * (size // share),
        input_output_aliases={len(given) - 1: 0},
        scratch_shapes=[pltpu.VMEM((size, emb_width), f32), pltpu.VMEM((size, width), bf16)],
        compiler_params=params(4 * size * width + 4 * size * emb_width),
        cost_estimate=cost(2 * rows * size * (width + 2 * emb_width), 2 * size * (width + 2 * emb_width)),
    )(*given)


def late_kernel(count, masks, summed, order_ref, *refs):
    tea_ref, emb_ref, proj_ref, before_ref = refs[:4]
    text_refs = refs[4 : 4 + count]
    refs = refs[4 + count :]
    if summed:
        texts_before_ref, refs = refs[0], refs[1:]
    give_ref, *keep_refs, out_ref, grads_ref, texts_ref = refs
    share = keep_refs[0].shape[0]
    join(text_refs, texts_ref)
    grads_ref[...] = texts_before_ref[...] if summed else jnp.zeros_like(grads_ref)
    for k in range(masks):
        blocks = [pl.ds(pl.multiple_of(order_ref[2 * k + place] * share, share), share) for place in range(2)]
        joined = [jnp.concatenate([ref[rows, :] for rows in blocks]) for ref in (tea_ref, emb_ref)]
        grads = pair_tile(*joined, texts_ref, grads_ref)
        for place, rows in enumerate(blocks):
            whole = grads[place * share : (place + 1) * share] + before_ref[rows, :]
            floats = proj_ref[rows, :].astype(f32)
            inverse = inverse_length(floats)
            unit = floats * inverse
            along = jnp.sum(unit * whole, axis=1, keepdims=True)
            part = ((whole - unit * along) * inverse).astype(bf16)
            if place == 0:
                give_ref[pl.ds(k * share, share), :] = part
            else:
                keep_refs[k][...] = part
    out_ref[...] = grads_ref[...].astype(out_ref.dtype)


def late(order, tea_emb, emb, proj, before, texts, texts_before, share):
    tea_width, emb_width = tea_emb.shape[1], emb.shape[1]
    width = texts[0].shape[1]
    count = len(texts)
    size = sum(part.shape[0] for part in texts)
    masks = order.shape[0] // 2
    summed = texts_before is not None
    given = [pinned(tea_emb), pinned(emb), pinned(proj), pinned(before), *texts]
    given += [texts_before] if summed else []
    return pl.pallas_call(
        functools.partial(late_kernel, count, masks, summed),
        in_specs=[pl.BlockSpec(memory_space=pltpu.SMEM)] + [resident] * len(given),
        out_specs=[resident] * (masks + 2),
        out_shape=[jax.ShapeDtypeStruct((masks * share, emb_width), bf16)]
        + [jax.ShapeDtypeStruct((share, emb_width), bf16)] * masks
        + [jax.ShapeDtypeStruct((size, emb_width), bf16 if summed else f32)],
        scratch_shapes=[pltpu.VMEM((size, emb_width), f32), pltpu.VMEM((size, width), bf16)],
        compiler_params=params(),
        cost_estimate=cost(
            4 * masks * share * size * (width + 2 * emb_width), 4 * masks * share * emb_width
        ),
    )(order, *given)


def merge_kernel(take_ref, *refs):
    for k in range(len(refs) // 2):
        rows = refs[k].shape[0]
        refs[k + len(refs) // 2][...] = refs[k][...] + take_ref[pl.ds(k * rows, rows), :]


def merged(take, keeps):
    size = take.size
    return pl.pallas_call(
        merge_kernel,
        out_shape=[jax.ShapeDtypeStruct(keep.shape, keep.dtype) for keep in keeps],
        compiler_params=params(),
        cost_estimate=cost(0, 0),
    )(take, *keeps)


def head_kernel(order_ref, images_ref, *refs):
    (near_ref, far_ref, total_ref), part_refs = refs[-3:], refs[:-3]
    count, dp_count, rows, _ = near_ref.shape
    columns = dp_count * rows
    share = part_refs[0].shape[0]
    total = None
    for k in range(count):
        places = pl.ds(pl.multiple_of(order_ref[2 * k] * share, share), share)
        term = lax.dot_general(part_refs[k][...], images_ref[places, :], TN, preferred_element_type=f32)
        total = term if total is None else total + term
    total_ref[...] = total
    for k in range(count):
        for place, ref in enumerate((near_ref, far_ref)):
            start = pl.multiple_of(order_ref[2 * k + place] * columns, columns)
            block = total_ref[pl.ds(start, columns), :]
            for j in range(dp_count):
                ref[k, j, :, :] = block[j * rows : (j + 1) * rows].astype(bf16)


def head_parts(order, images, parts, columns, dp_count):
    share, width = parts[0].shape
    depth = images.shape[1]
    count = len(parts)
    piece = jax.ShapeDtypeStruct((count, dp_count, columns // dp_count, depth), bf16)
    return pl.pallas_call(
        head_kernel,
        in_specs=[pl.BlockSpec(memory_space=pltpu.SMEM)] + [resident] * (1 + count),
        out_specs=[resident] * 2,
        out_shape=(piece, piece),
        scratch_shapes=[pltpu.VMEM((width, depth), f32)],
        compiler_params=params(),
        cost_estimate=cost(0, 0),
    )(order, pinned(images), *parts)


def split_kernel(gates, order_ref, near_ref, far_ref, *refs):
    for k, ref in enumerate(refs[gates:]):
        for j in range(near_ref.shape[0]):
            ref[j, :, :] = near_ref[j, order_ref[k]] + far_ref[j, order_ref[k]]


def split(order, near, far, gates):
    count, dp_count, rows, depth = near.shape
    return pl.pallas_call(
        functools.partial(split_kernel, len(gates)),
        in_specs=[pl.BlockSpec(memory_space=pltpu.SMEM)]
        + [resident] * 2
        + [pl.BlockSpec(memory_space=pl.ANY)] * len(gates),
        out_specs=[resident] * dp_count,
        out_shape=[jax.ShapeDtypeStruct((count, rows, depth), bf16)] * dp_count,
        compiler_params=params(),
        cost_estimate=cost(0, 0),
    )(order, near, far, *gates)


def head_result_kernel(scale, order_ref, *refs):
    pieces, (out_ref, total_ref) = refs[:-2], refs[-2:]
    for k, ref in enumerate(pieces):
        total_ref[order_ref[k]] = ref[...].astype(f32)
    rows = total_ref.shape[1]
    total = jnp.concatenate([total_ref[k] for k in range(len(pieces))])
    out_ref[...] = total.T * scale


def head_result(order, pieces, scale):
    rows, depth = pieces[0].shape
    count = len(pieces)
    return pl.pallas_call(
        functools.partial(head_result_kernel, scale),
        in_specs=[pl.BlockSpec(memory_space=pltpu.SMEM)] + [resident] * count,
        out_specs=resident,
        out_shape=jax.ShapeDtypeStruct((depth, count * rows), f32),
        scratch_shapes=[pltpu.VMEM((count, rows, depth), f32)],
        compiler_params=params(),
        cost_estimate=cost(0, 0),
    )(order, *pieces)


def text_result_kernel(scale, stu_ref, own_ref, *refs):
    total = own_ref[...]
    for ref in refs[:-1]:
        total += ref[...].astype(f32)
    stu = stu_ref[...].astype(f32)
    inverse = inverse_length(stu)
    unit = stu * inverse
    along = jnp.sum(unit * total, axis=1, keepdims=True)
    refs[-1][...] = (total - unit * along) * (inverse * scale)


def text_result(stu_txt, own, got, scale):
    rows, width = own.shape
    return pl.pallas_call(
        functools.partial(text_result_kernel, scale),
        out_shape=jax.ShapeDtypeStruct((rows, width), f32),
        compiler_params=params(),
        cost_estimate=cost(0, 0),
    )(stu_txt, own, *got)


def images_kernel(scale, *refs):
    part_refs, head_ref, out_ref, mark_ref = refs[:-3], *refs[-3:]
    total = part_refs[0][...].astype(f32)
    for ref in part_refs[1:]:
        total += ref[...].astype(f32)
    out_ref[...] = scale * jnp.dot(total.astype(bf16), head_ref[...], preferred_element_type=f32)
    mark_ref[...] = jnp.zeros_like(mark_ref)


def image_grads(parts, head, scale):
    share, width = parts[0].shape
    depth = head.shape[1]
    return pl.pallas_call(
        functools.partial(images_kernel, scale),
        out_shape=(jax.ShapeDtypeStruct((share, depth), f32), jax.ShapeDtypeStruct((8, 128), f32)),
        compiler_params=params(),
        cost_estimate=cost(0, 0),
    )(*parts, head)


def per_device(images, head, tea_img, stu_txt, tea_txt):
    dp_count = lax.axis_size("dp")
    tensor_count = lax.axis_size("tensor")
    rank = lax.axis_index("tensor")
    rows = images.shape[0]
    columns = head.shape[1]
    share = rows // tensor_count
    half = share // 2
    pairs = tensor_count // 2
    bits = dp_count.bit_length() - 1
    factor = 0.5 * logit_scale * loss_scale / (rows * dp_count)

    texts = {0: text_halves(tea_txt, stu_txt)}
    for mask in sorted(range(1, dp_count), key=lambda m: (m.bit_count(), m)):
        first, last = mask & -mask, 1 << (mask.bit_length() - 1)
        texts[mask] = [swap(texts[mask ^ last][0], "dp", last), swap(texts[mask ^ first][1], "dp", first)]

    head_t = head.T
    tea_emb, target, held_images = teacher_emb(tea_img, images, *texts[0])
    near = stacked([head_t] + [swap(head_t, "tensor", 2 * k) for k in range(1, pairs)])
    far = swap(near, "tensor", 1)
    order = jnp.stack([rank ^ (2 * k + place) for k in range(pairs) for place in range(2)]).astype(jnp.int32)
    proj, emb, head_full = projections(order, held_images, near, far, tea_emb, target)

    text_grads = {}
    image_part, text_grads[0] = own_texts(target, emb, *texts[0], tea_emb)
    middle = list(range(1, dp_count - 1))
    given = [part for mask in middle for part in texts[mask]]
    image_part, *block_sums = early(tea_emb, emb, given, image_part, share)
    text_grads.update(zip(middle, block_sums))
    last = dp_count - 1
    grads = None
    parts = {}
    for masks in (list(range(pairs // 2, pairs))[::-1], list(range(pairs // 2))[::-1]):
        chosen = jnp.stack([order[2 * k + place] for k in masks for place in (1, 0)])
        give, *keeps, grads = late(chosen, tea_emb, emb, proj, image_part, texts[last], grads, share)
        parts.update(zip(masks, merged(swap(give, "tensor", 1), keeps)))
    text_grads[last] = grads

    near, far = head_parts(order, held_images, [parts[mask] for mask in range(pairs)], columns, dp_count)
    far = swap(far, "tensor", 1)
    dp_order = jnp.stack([lax.axis_index("dp") ^ mask for mask in range(dp_count)]).astype(jnp.int32)
    got = {mask: swap(text_grads[mask], "dp", mask) for mask in range(1, dp_count)}
    pieces = split(dp_order, near, far, [])
    pieces = [pieces[0]] + [swap(pieces[mask], "dp", mask) for mask in range(1, dp_count)]

    for bit in range(pairs.bit_length() - 1):
        sent = [mask for mask in sorted(parts) if mask >> bit & 1 and mask != 1 << bit]
        passed = [swap(parts.pop(mask), "tensor", 2 << bit) for mask in sent]
        targets = [mask ^ 1 << bit for mask in sent]
        if targets:
            parts.update(zip(targets, sums([[parts[mask], block] for mask, block in zip(targets, passed)], [far])))
    arrived = [swap(parts[1 << bit], "tensor", 2 << bit) for bit in range(pairs.bit_length() - 1)]
    grad_images, images_mark = image_grads([parts[0]] + arrived, head_full, factor)

    held, count = pieces, pairs
    while count > 1:
        low, high = folded(held)
        held = [low, swap(high, "tensor", count)]
        count //= 2
    (own,) = sums([held], arrived + [got[mask] for mask in middle])
    own = own[0]
    shares = [own] + [swap(own, "dp", mask) for mask in range(1, dp_count)]
    grad_head = head_result(dp_order, shares, factor)

    grad_text = text_result(stu_txt, text_grads[0], list(got.values()), factor / half_scale)
    return (grad_images, grad_head, grad_text)


def solution(mesh):
    placed = (
        P("dp", None),
        P(None, "tensor"),
        P("dp", None),
        P(("dp", "tensor"), None),
        P(("dp", "tensor"), None),
    )
    return jax.shard_map(
        per_device,
        mesh=mesh,
        in_specs=placed,
        out_specs=(P(("dp", "tensor"), None), P(None, "tensor"), P(("dp", "tensor"), None)),
        check_vma=False,
    )
```

```python
import functools
import math
import jax
import jax.numpy as jnp
from jax import lax
from jax.experimental import pallas as pl
from jax.experimental.pallas import tpu as pltpu
from jax.sharding import PartitionSpec as P

logit_scale = 64.0
logit_bias = -2.0
loss_scale = 65536.0
half_scale = 0.5 * logit_scale
half_bias = 0.5 * logit_bias
bf16 = jnp.bfloat16
f32 = jnp.float32
NT = (((1,), (1,)), ((), ()))
TN = (((0,), (0,)), ((), ()))


def params(held=0):
    return pltpu.CompilerParams(vmem_limit_bytes=held + 10 * 1024 * 1024)


resident = pl.BlockSpec(memory_space=pltpu.VMEM)


def pinned(value):
    return pltpu.with_memory_space_constraint(value, pltpu.VMEM)


def cost(flops, moved, trans=0):
    return pl.CostEstimate(flops=int(flops), bytes_accessed=int(moved), transcendentals=int(trans))


def swap(value, axis, mask):
    count = lax.axis_size(axis)
    return lax.ppermute(value, axis, [(source, source ^ mask) for source in range(count)])


def inverse_length(floats):
    return lax.rsqrt(jnp.sum(floats * floats, axis=1, keepdims=True) + 1e-06)


def in_hbm(value):
    return pltpu.with_memory_space_constraint(value, pltpu.HBM)


def stack_kernel(*refs):
    piece_refs, out_ref = refs[:-1], refs[-1]
    for k, ref in enumerate(piece_refs):
        out_ref[k, :, :] = ref[...]


def stacked(pieces):
    shape = (len(pieces), *pieces[0].shape)
    return pl.pallas_call(
        stack_kernel,
        in_specs=[resident] * len(pieces),
        out_specs=resident,
        out_shape=jax.ShapeDtypeStruct(shape, pieces[0].dtype),
        compiler_params=params(),
        cost_estimate=cost(0, 4 * math.prod(shape)),
    )(*pieces)


def sum_kernel(groups, *refs):
    start = 0
    for terms, out_ref in zip(groups, refs[-len(groups) :]):
        total = refs[start][...].astype(f32)
        for ref in refs[start + 1 : start + terms]:
            total += ref[...].astype(f32)
        out_ref[...] = total.astype(bf16)
        start += terms


def sums(groups, gates):
    given = [term for group in groups for term in group]
    size = sum(math.prod(term.shape) for term in given)
    return pl.pallas_call(
        functools.partial(sum_kernel, [len(group) for group in groups]),
        in_specs=[resident] * len(given) + [pl.BlockSpec(memory_space=pl.ANY)] * len(gates),
        out_specs=[resident] * len(groups),
        out_shape=[jax.ShapeDtypeStruct(group[0].shape, bf16) for group in groups],
        compiler_params=params(),
        cost_estimate=cost(0, 0),
    )(*given, *gates)


def fold_kernel(*refs):
    terms, (low_ref, high_ref) = refs[:-2], refs[-2:]
    half = low_ref.shape[0]
    for k, out_ref in enumerate((low_ref, high_ref)):
        total = terms[0][k * half : (k + 1) * half].astype(f32)
        for ref in terms[1:]:
            total += ref[k * half : (k + 1) * half].astype(f32)
        out_ref[...] = total.astype(bf16)


def folded(terms):
    count, *rest = terms[0].shape
    size = len(terms) * math.prod(terms[0].shape)
    return pl.pallas_call(
        fold_kernel,
        in_specs=[resident] * len(terms),
        out_specs=[resident] * 2,
        out_shape=[jax.ShapeDtypeStruct((count // 2, *rest), bf16)] * 2,
        compiler_params=params(),
        cost_estimate=cost(0, 0),
    )(*terms)


def text_kernel(tea_ref, stu_ref, low_ref, high_ref):
    tea_width = tea_ref.shape[1]
    for place, out_ref in enumerate((low_ref, high_ref)):

        @pl.when(pl.program_id(0) == place)
        def _(out_ref=out_ref):
            tea = tea_ref[...].astype(f32)
            out_ref[:, :tea_width] = (tea * inverse_length(tea)).astype(bf16)
            stu = stu_ref[...].astype(f32)
            out_ref[:, tea_width:] = (stu * inverse_length(stu)).astype(bf16)


def text_halves(tea_txt, stu_txt):
    share, tea_width = tea_txt.shape
    stu_width = stu_txt.shape[1]
    half = share // 2
    part = jax.ShapeDtypeStruct((half, tea_width + stu_width), bf16)
    row = lambda width: pl.BlockSpec((half, width), lambda i: (i, 0))
    return pl.pallas_call(
        text_kernel,
        grid=(2,),
        in_specs=[row(tea_width), row(stu_width)],
        out_specs=[resident] * 2,
        out_shape=(part, part),
        compiler_params=params(),
        cost_estimate=cost(4 * share * tea_width, 4 * share * tea_width),
    )(in_hbm(tea_txt), in_hbm(stu_txt))


def teacher_kernel(tea_ref, images_ref, low_ref, high_ref, emb_ref, target_ref, held_ref):
    chunk, width = tea_ref.shape
    rows = pl.ds(pl.multiple_of(pl.program_id(0) * chunk, chunk), chunk)
    tea = tea_ref[...].astype(f32)
    emb = (tea * inverse_length(tea)).astype(bf16) * half_scale
    emb_ref[rows, :] = emb
    half = low_ref.shape[0]
    for place, ref in enumerate((low_ref, high_ref)):
        target = lax.dot_general(emb, ref[:, :width], NT, preferred_element_type=f32)
        target_ref[rows, pl.ds(place * half, half)] = jnp.tanh(target + half_bias)
    held_ref[rows, :] = images_ref[...]


def teacher_emb(tea_img, images, low, high):
    rows, width = tea_img.shape
    depth = images.shape[1]
    chunk = math.gcd(rows, 512)
    size = 2 * low.shape[0]
    row = lambda width: pl.BlockSpec((chunk, width), lambda i: (i, 0))
    return pl.pallas_call(
        teacher_kernel,
        grid=(rows // chunk,),
        in_specs=[row(width), row(depth), resident, resident],
        out_specs=[resident] * 3,
        out_shape=(
            pltpu.VMEM((rows, width), bf16),
            pltpu.VMEM((rows, size), f32),
            pltpu.VMEM((rows, depth), bf16),
        ),
        compiler_params=params(),
        cost_estimate=cost(2 * rows * width * size, 2 * rows * width),
    )(in_hbm(tea_img), in_hbm(images), low, high)


def proj_kernel(order_ref, images_ref, near_ref, far_ref, _tea_ref, _target_ref, proj_ref, emb_ref, head_ref):
    count, columns = near_ref.shape[:2]
    size = images_ref.shape[0]
    chunk = math.gcd(size, 512)
    for k in range(count):
        for place, ref in enumerate((near_ref, far_ref)):
            start = pl.multiple_of(order_ref[2 * k + place] * columns, columns)
            head_ref[pl.ds(start, columns), :] = ref[k]
    for k in range(size // chunk):
        rows = pl.ds(k * chunk, chunk)
        proj = lax.dot_general(images_ref[rows, :], head_ref[...], NT, preferred_element_type=f32).astype(bf16)
        floats = proj.astype(f32)
        proj_ref[rows, :] = proj
        emb_ref[rows, :] = (floats * inverse_length(floats)).astype(bf16) * half_scale


def projections(order, images, near, far, *held):
    rows, depth = images.shape
    count, columns, _ = near.shape
    width = 2 * count * columns
    return pl.pallas_call(
        proj_kernel,
        in_specs=[pl.BlockSpec(memory_space=pltpu.SMEM)] + [resident] * (3 + len(held)),
        out_specs=[resident, resident, resident],
        out_shape=(
            pltpu.VMEM((rows, width), bf16),
            pltpu.VMEM((rows, width), bf16),
            jax.ShapeDtypeStruct((width, depth), bf16),
        ),
        compiler_params=params(),
        cost_estimate=cost(2 * rows * depth * width, 2 * rows * depth),
    )(order, pinned(images), near, far, *map(pinned, held))


def pair_tile(tea, emb, texts, grads_ref, target=None):
    stu = texts[:, -emb.shape[1] :]
    if target is None:
        target = lax.dot_general(tea, texts[:, : tea.shape[1]], NT, preferred_element_type=f32)
        target = jnp.tanh(target + half_bias)
    student = lax.dot_general(emb, stu, NT, preferred_element_type=f32)
    coef = (jnp.tanh(student + half_bias) - target).astype(bf16)
    part = jnp.dot(coef, stu, preferred_element_type=f32)
    grads_ref[...] += lax.dot_general(coef, emb, TN, preferred_element_type=f32)
    return part


def own_kernel(target_ref, emb_ref, low_ref, high_ref, _tea_ref, out_ref, grads_ref, texts_ref):
    width = emb_ref.shape[1]
    half = low_ref.shape[0]
    texts_ref[pl.ds(0, half), :] = low_ref[:, -width:]
    texts_ref[pl.ds(half, half), :] = high_ref[:, -width:]
    size = emb_ref.shape[0]
    chunk = math.gcd(size, 512)
    grads_ref[...] = jnp.zeros_like(grads_ref)
    for k in range(size // chunk):
        rows = pl.ds(k * chunk, chunk)
        out_ref[rows, :] = pair_tile(None, emb_ref[rows, :], texts_ref, grads_ref, target_ref[rows, :])


def own_texts(target, emb, low, high, tea_emb):
    rows, width = emb.shape
    size = target.shape[1]
    return pl.pallas_call(
        own_kernel,
        in_specs=[resident] * 5,
        out_specs=[resident, resident],
        out_shape=(pltpu.VMEM((rows, width), f32), jax.ShapeDtypeStruct((size, width), f32)),
        scratch_shapes=[pltpu.VMEM((size, width), bf16)],
        compiler_params=params(),
        cost_estimate=cost(6 * rows * size * width, 6 * size * width),
    )(pinned(target), pinned(emb), low, high, pinned(tea_emb))


def join(text_refs, out_ref):
    start = 0
    for ref in text_refs:
        out_ref[pl.ds(start, ref.shape[0]), :] = ref[...]
        start += ref.shape[0]


def early_kernel(count, *refs):
    tea_ref, emb_ref = refs[:2]
    text_refs = refs[2 : 2 + count]
    before_ref, out_ref, *sum_refs, grads_ref, texts_ref = refs[2 + count :]
    size = tea_ref.shape[0]
    chunk = math.gcd(size, 512)
    join(text_refs, texts_ref)
    grads_ref[...] = jnp.zeros_like(grads_ref)
    for k in range(size // chunk):
        rows = pl.ds(k * chunk, chunk)
        part = pair_tile(tea_ref[rows, :], emb_ref[rows, :], texts_ref, grads_ref)
        out_ref[rows, :] = part + before_ref[rows, :]
    share = grads_ref.shape[0] // len(sum_refs)
    for k, ref in enumerate(sum_refs):
        ref[...] = grads_ref[pl.ds(k * share, share), :].astype(bf16)


def early(tea_emb, emb, texts, before, share):
    rows = tea_emb.shape[0]
    emb_width = emb.shape[1]
    width = texts[0].shape[1]
    count = len(texts)
    size = sum(part.shape[0] for part in texts)
    given = [pinned(tea_emb), pinned(emb), *texts, pinned(before)]
    return pl.pallas_call(
        functools.partial(early_kernel, count),
        in_specs=[resident] * len(given),
        out_specs=[resident] * (1 + size // share),
        out_shape=[pltpu.VMEM((rows, emb_width), f32)]
        + [jax.ShapeDtypeStruct((share, emb_width), bf16)] * (size // share),
        input_output_aliases={len(given) - 1: 0},
        scratch_shapes=[pltpu.VMEM((size, emb_width), f32), pltpu.VMEM((size, width), bf16)],
        compiler_params=params(4 * size * width + 4 * size * emb_width),
        cost_estimate=cost(2 * rows * size * (width + 2 * emb_width), 2 * size * (width + 2 * emb_width)),
    )(*given)


def late_kernel(count, masks, summed, order_ref, *refs):
    tea_ref, emb_ref, proj_ref, before_ref = refs[:4]
    text_refs = refs[4 : 4 + count]
    refs = refs[4 + count :]
    if summed:
        texts_before_ref, refs = refs[0], refs[1:]
    give_ref, *keep_refs, out_ref, grads_ref, texts_ref = refs
    share = keep_refs[0].shape[0]
    join(text_refs, texts_ref)
    grads_ref[...] = texts_before_ref[...] if summed else jnp.zeros_like(grads_ref)
    for k in range(masks):
        blocks = [pl.ds(pl.multiple_of(order_ref[2 * k + place] * share, share), share) for place in range(2)]
        joined = [jnp.concatenate([ref[rows, :] for rows in blocks]) for ref in (tea_ref, emb_ref)]
        grads = pair_tile(*joined, texts_ref, grads_ref)
        for place, rows in enumerate(blocks):
            whole = grads[place * share : (place + 1) * share] + before_ref[rows, :]
            floats = proj_ref[rows, :].astype(f32)
            inverse = inverse_length(floats)
            unit = floats * inverse
            along = jnp.sum(unit * whole, axis=1, keepdims=True)
            part = ((whole - unit * along) * inverse).astype(bf16)
            if place == 0:
                give_ref[pl.ds(k * share, share), :] = part
            else:
                keep_refs[k][...] = part
    out_ref[...] = grads_ref[...].astype(out_ref.dtype)


def late(order, tea_emb, emb, proj, before, texts, texts_before, share):
    tea_width, emb_width = tea_emb.shape[1], emb.shape[1]
    width = texts[0].shape[1]
    count = len(texts)
    size = sum(part.shape[0] for part in texts)
    masks = order.shape[0] // 2
    summed = texts_before is not None
    given = [pinned(tea_emb), pinned(emb), pinned(proj), pinned(before), *texts]
    given += [texts_before] if summed else []
    return pl.pallas_call(
        functools.partial(late_kernel, count, masks, summed),
        in_specs=[pl.BlockSpec(memory_space=pltpu.SMEM)] + [resident] * len(given),
        out_specs=[resident] * (masks + 2),
        out_shape=[jax.ShapeDtypeStruct((masks * share, emb_width), bf16)]
        + [jax.ShapeDtypeStruct((share, emb_width), bf16)] * masks
        + [jax.ShapeDtypeStruct((size, emb_width), bf16)],
        scratch_shapes=[pltpu.VMEM((size, emb_width), f32), pltpu.VMEM((size, width), bf16)],
        compiler_params=params(),
        cost_estimate=cost(
            4 * masks * share * size * (width + 2 * emb_width), 4 * masks * share * emb_width
        ),
    )(order, *given)


def head_kernel(order_ref, images_ref, take_ref, *refs):
    count = (len(refs) - 3) // 2
    keep_refs, (near_ref, far_ref), part_refs, total_ref = refs[:count], refs[count : count + 2], refs[count + 2 : -1], refs[-1]
    _, dp_count, rows, _ = near_ref.shape
    columns = dp_count * rows
    share = keep_refs[0].shape[0]
    total = None
    for k in range(count):
        places = pl.ds(pl.multiple_of(order_ref[2 * k] * share, share), share)
        part = keep_refs[k][...] + take_ref[pl.ds((count - 1 - k) * share, share), :]
        part_refs[k][...] = part
        term = lax.dot_general(part, images_ref[places, :], TN, preferred_element_type=f32)
        total = term if total is None else total + term
    total_ref[...] = total
    for k in range(count):
        for place, ref in enumerate((near_ref, far_ref)):
            start = pl.multiple_of(order_ref[2 * k + place] * columns, columns)
            block = total_ref[pl.ds(start, columns), :]
            for j in range(dp_count):
                ref[k, j, :, :] = block[j * rows : (j + 1) * rows].astype(bf16)


def head_parts(order, images, take, keeps, columns, dp_count):
    share, width = keeps[0].shape
    depth = images.shape[1]
    count = len(keeps)
    piece = jax.ShapeDtypeStruct((count, dp_count, columns // dp_count, depth), bf16)
    return pl.pallas_call(
        head_kernel,
        in_specs=[pl.BlockSpec(memory_space=pltpu.SMEM)] + [resident] * (2 + count),
        out_specs=[resident] * (2 + count),
        out_shape=[piece] * 2 + [jax.ShapeDtypeStruct((share, width), bf16)] * count,
        scratch_shapes=[pltpu.VMEM((width, depth), f32)],
        compiler_params=params(),
        cost_estimate=cost(2 * count * share * width * depth, 4 * count * share * width),
    )(order, pinned(images), take, *keeps)


def split_kernel(gates, order_ref, near_ref, far_ref, *refs):
    for k, ref in enumerate(refs[gates:]):
        for j in range(near_ref.shape[0]):
            ref[j, :, :] = near_ref[j, order_ref[k]] + far_ref[j, order_ref[k]]


def split(order, near, far, gates):
    count, dp_count, rows, depth = near.shape
    return pl.pallas_call(
        functools.partial(split_kernel, len(gates)),
        in_specs=[pl.BlockSpec(memory_space=pltpu.SMEM)]
        + [resident] * 2
        + [pl.BlockSpec(memory_space=pl.ANY)] * len(gates),
        out_specs=[resident] * dp_count,
        out_shape=[jax.ShapeDtypeStruct((count, rows, depth), bf16)] * dp_count,
        compiler_params=params(),
        cost_estimate=cost(0, 0),
    )(order, near, far, *gates)


def head_result_kernel(scale, order_ref, *refs):
    pieces, (out_ref, total_ref) = refs[:-2], refs[-2:]
    for k, ref in enumerate(pieces):
        total_ref[order_ref[k]] = ref[...].astype(f32)
    rows = total_ref.shape[1]
    total = jnp.concatenate([total_ref[k] for k in range(len(pieces))])
    out_ref[...] = total.T * scale


def head_result(order, pieces, scale):
    rows, depth = pieces[0].shape
    count = len(pieces)
    return pl.pallas_call(
        functools.partial(head_result_kernel, scale),
        in_specs=[pl.BlockSpec(memory_space=pltpu.SMEM)] + [resident] * count,
        out_specs=resident,
        out_shape=jax.ShapeDtypeStruct((depth, count * rows), f32),
        scratch_shapes=[pltpu.VMEM((count, rows, depth), f32)],
        compiler_params=params(),
        cost_estimate=cost(0, 0),
    )(order, *pieces)


def text_result_kernel(scale, stu_ref, own_ref, *refs):
    total = own_ref[...]
    for ref in refs[:-1]:
        total += ref[...].astype(f32)
    stu = stu_ref[...].astype(f32)
    inverse = inverse_length(stu)
    unit = stu * inverse
    along = jnp.sum(unit * total, axis=1, keepdims=True)
    refs[-1][...] = (total - unit * along) * (inverse * scale)


def text_result(stu_txt, own, got, scale):
    rows, width = own.shape
    return pl.pallas_call(
        functools.partial(text_result_kernel, scale),
        out_shape=jax.ShapeDtypeStruct((rows, width), f32),
        compiler_params=params(),
        cost_estimate=cost(0, 0),
    )(stu_txt, own, *got)


def images_kernel(scale, *refs):
    part_refs, head_ref, out_ref, mark_ref = refs[:-3], *refs[-3:]
    total = part_refs[0][...].astype(f32)
    for ref in part_refs[1:]:
        total += ref[...].astype(f32)
    out_ref[...] = scale * jnp.dot(total.astype(bf16), head_ref[...], preferred_element_type=f32)
    mark_ref[...] = jnp.zeros_like(mark_ref)


def image_grads(parts, head, scale):
    share, width = parts[0].shape
    depth = head.shape[1]
    return pl.pallas_call(
        functools.partial(images_kernel, scale),
        out_shape=(jax.ShapeDtypeStruct((share, depth), f32), jax.ShapeDtypeStruct((8, 128), f32)),
        compiler_params=params(),
        cost_estimate=cost(0, 0),
    )(*parts, head)


def per_device(images, head, tea_img, stu_txt, tea_txt):
    dp_count = lax.axis_size("dp")
    tensor_count = lax.axis_size("tensor")
    rank = lax.axis_index("tensor")
    rows = images.shape[0]
    columns = head.shape[1]
    share = rows // tensor_count
    half = share // 2
    pairs = tensor_count // 2
    bits = dp_count.bit_length() - 1
    factor = 0.5 * logit_scale * loss_scale / (rows * dp_count)

    texts = {0: text_halves(tea_txt, stu_txt)}
    for mask in sorted(range(1, dp_count), key=lambda m: (m.bit_count(), m)):
        first, last = mask & -mask, 1 << (mask.bit_length() - 1)
        texts[mask] = [swap(texts[mask ^ last][0], "dp", last), swap(texts[mask ^ first][1], "dp", first)]

    head_t = head.T
    tea_emb, target, held_images = teacher_emb(tea_img, images, *texts[0])
    near = stacked([head_t] + [swap(head_t, "tensor", 2 * k) for k in range(1, pairs)])
    far = swap(near, "tensor", 1)
    order = jnp.stack([rank ^ (2 * k + place) for k in range(pairs) for place in range(2)]).astype(jnp.int32)
    proj, emb, head_full = projections(order, held_images, near, far, tea_emb, target)

    text_grads = {}
    image_part, text_grads[0] = own_texts(target, emb, *texts[0], tea_emb)
    middle = list(range(1, dp_count - 1))
    given = [part for mask in middle for part in texts[mask]]
    image_part, *block_sums = early(tea_emb, emb, given, image_part, share)
    text_grads.update(zip(middle, block_sums))
    last = dp_count - 1
    chosen = jnp.stack([order[2 * k + place] for k in range(pairs)[::-1] for place in (1, 0)])
    give, *keeps, grads = late(chosen, tea_emb, emb, proj, image_part, texts[last], None, share)
    keeps = dict(zip(range(pairs)[::-1], keeps))
    take = swap(give, "tensor", 1)
    text_grads[last] = grads

    near, far, *parts = head_parts(order, held_images, take, [keeps[mask] for mask in range(pairs)], columns, dp_count)
    parts = dict(enumerate(parts))
    far = swap(far, "tensor", 1)
    dp_order = jnp.stack([lax.axis_index("dp") ^ mask for mask in range(dp_count)]).astype(jnp.int32)
    pieces = split(dp_order, near, far, [])
    pieces = [pieces[0]] + [swap(pieces[mask], "dp", mask) for mask in range(1, dp_count)]

    for bit in range(pairs.bit_length() - 1):
        sent = [mask for mask in sorted(parts) if mask >> bit & 1 and mask != 1 << bit]
        passed = [swap(parts.pop(mask), "tensor", 2 << bit) for mask in sent]
        targets = [mask ^ 1 << bit for mask in sent]
        if targets:
            parts.update(zip(targets, sums([[parts[mask], block] for mask, block in zip(targets, passed)], [far])))
    leaving = sums([[text_grads[mask]] for mask in range(1, dp_count)], [parts[pairs // 2]])
    got = {mask: swap(block, "dp", mask) for mask, block in zip(range(1, dp_count), leaving)}
    arrived = [swap(parts[1 << bit], "tensor", 2 << bit) for bit in range(pairs.bit_length() - 1)]
    grad_images, images_mark = image_grads([parts[0]] + arrived, head_full, factor)

    held, count = pieces, pairs
    while count > 1:
        low, high = folded(held)
        held = [low, swap(high, "tensor", count)]
        count //= 2
    (own,) = sums([held], arrived)
    own = own[0]
    shares = [own] + [swap(own, "dp", mask) for mask in range(1, dp_count)]
    grad_head = head_result(dp_order, shares, factor)

    grad_text = text_result(stu_txt, text_grads[0], list(got.values()), factor / half_scale)
    return (grad_images, grad_head, grad_text)


def solution(mesh):
    placed = (
        P("dp", None),
        P(None, "tensor"),
        P("dp", None),
        P(("dp", "tensor"), None),
        P(("dp", "tensor"), None),
    )
    return jax.shard_map(
        per_device,
        mesh=mesh,
        in_specs=placed,
        out_specs=(P(("dp", "tensor"), None), P(None, "tensor"), P(("dp", "tensor"), None)),
        check_vma=False,
    )
```

```python
import functools
import math
import jax
import jax.numpy as jnp
from jax import lax
from jax.experimental import pallas as pl
from jax.experimental.pallas import tpu as pltpu
from jax.sharding import PartitionSpec as P

logit_scale = 64.0
logit_bias = -2.0
loss_scale = 65536.0
half_scale = 0.5 * logit_scale
half_bias = 0.5 * logit_bias
bf16 = jnp.bfloat16
f32 = jnp.float32
NT = (((1,), (1,)), ((), ()))
TN = (((0,), (0,)), ((), ()))


def params(held=0):
    return pltpu.CompilerParams(vmem_limit_bytes=held + 10 * 1024 * 1024)


resident = pl.BlockSpec(memory_space=pltpu.VMEM)


def pinned(value):
    return pltpu.with_memory_space_constraint(value, pltpu.VMEM)


def cost(flops, moved, trans=0):
    return pl.CostEstimate(flops=int(flops), bytes_accessed=int(moved), transcendentals=int(trans))


def swap(value, axis, mask):
    count = lax.axis_size(axis)
    return lax.ppermute(value, axis, [(source, source ^ mask) for source in range(count)])


def inverse_length(floats):
    return lax.rsqrt(jnp.sum(floats * floats, axis=1, keepdims=True) + 1e-06)


def in_hbm(value):
    return pltpu.with_memory_space_constraint(value, pltpu.HBM)


def stack_kernel(*refs):
    piece_refs, out_ref = refs[:-1], refs[-1]
    for k, ref in enumerate(piece_refs):
        out_ref[k, :, :] = ref[...]


def stacked(pieces):
    shape = (len(pieces), *pieces[0].shape)
    return pl.pallas_call(
        stack_kernel,
        in_specs=[resident] * len(pieces),
        out_specs=resident,
        out_shape=jax.ShapeDtypeStruct(shape, pieces[0].dtype),
        compiler_params=params(),
        cost_estimate=cost(0, 4 * math.prod(shape)),
    )(*pieces)


def sum_kernel(groups, *refs):
    start = 0
    for terms, out_ref in zip(groups, refs[-len(groups) :]):
        total = refs[start][...].astype(f32)
        for ref in refs[start + 1 : start + terms]:
            total += ref[...].astype(f32)
        out_ref[...] = total.astype(bf16)
        start += terms


def sums(groups, gates):
    given = [term for group in groups for term in group]
    size = sum(math.prod(term.shape) for term in given)
    return pl.pallas_call(
        functools.partial(sum_kernel, [len(group) for group in groups]),
        in_specs=[resident] * len(given) + [pl.BlockSpec(memory_space=pl.ANY)] * len(gates),
        out_specs=[resident] * len(groups),
        out_shape=[jax.ShapeDtypeStruct(group[0].shape, bf16) for group in groups],
        compiler_params=params(),
        cost_estimate=cost(0, 0),
    )(*given, *gates)


def fold_kernel(*refs):
    terms, (low_ref, high_ref) = refs[:-2], refs[-2:]
    half = low_ref.shape[0]
    for k, out_ref in enumerate((low_ref, high_ref)):
        total = terms[0][k * half : (k + 1) * half].astype(f32)
        for ref in terms[1:]:
            total += ref[k * half : (k + 1) * half].astype(f32)
        out_ref[...] = total.astype(bf16)


def folded(terms):
    count, *rest = terms[0].shape
    size = len(terms) * math.prod(terms[0].shape)
    return pl.pallas_call(
        fold_kernel,
        in_specs=[resident] * len(terms),
        out_specs=[resident] * 2,
        out_shape=[jax.ShapeDtypeStruct((count // 2, *rest), bf16)] * 2,
        compiler_params=params(),
        cost_estimate=cost(0, 0),
    )(*terms)


def text_kernel(tea_ref, stu_ref, low_ref, high_ref):
    tea_width = tea_ref.shape[1]
    for place, out_ref in enumerate((low_ref, high_ref)):

        @pl.when(pl.program_id(0) == place)
        def _(out_ref=out_ref):
            tea = tea_ref[...].astype(f32)
            out_ref[:, :tea_width] = (tea * inverse_length(tea)).astype(bf16)
            stu = stu_ref[...].astype(f32)
            out_ref[:, tea_width:] = (stu * inverse_length(stu)).astype(bf16)


def text_halves(tea_txt, stu_txt):
    share, tea_width = tea_txt.shape
    stu_width = stu_txt.shape[1]
    half = share // 2
    part = jax.ShapeDtypeStruct((half, tea_width + stu_width), bf16)
    row = lambda width: pl.BlockSpec((half, width), lambda i: (i, 0))
    return pl.pallas_call(
        text_kernel,
        grid=(2,),
        in_specs=[row(tea_width), row(stu_width)],
        out_specs=[resident] * 2,
        out_shape=(part, part),
        compiler_params=params(),
        cost_estimate=cost(4 * share * tea_width, 4 * share * tea_width),
    )(in_hbm(tea_txt), in_hbm(stu_txt))


def teacher_kernel(tea_ref, images_ref, low_ref, high_ref, emb_ref, target_ref, held_ref):
    chunk, width = tea_ref.shape
    rows = pl.ds(pl.multiple_of(pl.program_id(0) * chunk, chunk), chunk)
    tea = tea_ref[...].astype(f32)
    emb = (tea * inverse_length(tea)).astype(bf16) * half_scale
    emb_ref[rows, :] = emb
    half = low_ref.shape[0]
    for place, ref in enumerate((low_ref, high_ref)):
        target = lax.dot_general(emb, ref[:, :width], NT, preferred_element_type=f32)
        target_ref[rows, pl.ds(place * half, half)] = jnp.tanh(target + half_bias)
    held_ref[rows, :] = images_ref[...]


def teacher_emb(tea_img, images, low, high):
    rows, width = tea_img.shape
    depth = images.shape[1]
    chunk = math.gcd(rows, 512)
    size = 2 * low.shape[0]
    row = lambda width: pl.BlockSpec((chunk, width), lambda i: (i, 0))
    return pl.pallas_call(
        teacher_kernel,
        grid=(rows // chunk,),
        in_specs=[row(width), row(depth), resident, resident],
        out_specs=[resident] * 3,
        out_shape=(
            pltpu.VMEM((rows, width), bf16),
            pltpu.VMEM((rows, size), f32),
            pltpu.VMEM((rows, depth), bf16),
        ),
        compiler_params=params(),
        cost_estimate=cost(2 * rows * width * size, 2 * rows * width),
    )(in_hbm(tea_img), in_hbm(images), low, high)


def proj_kernel(order_ref, images_ref, near_ref, far_ref, _tea_ref, _target_ref, proj_ref, emb_ref, head_ref):
    count, columns = near_ref.shape[:2]
    size = images_ref.shape[0]
    chunk = math.gcd(size, 512)
    for k in range(count):
        for place, ref in enumerate((near_ref, far_ref)):
            start = pl.multiple_of(order_ref[2 * k + place] * columns, columns)
            head_ref[pl.ds(start, columns), :] = ref[k]
    for k in range(size // chunk):
        rows = pl.ds(k * chunk, chunk)
        proj = lax.dot_general(images_ref[rows, :], head_ref[...], NT, preferred_element_type=f32).astype(bf16)
        floats = proj.astype(f32)
        proj_ref[rows, :] = proj
        emb_ref[rows, :] = (floats * inverse_length(floats)).astype(bf16) * half_scale


def projections(order, images, near, far, *held):
    rows, depth = images.shape
    count, columns, _ = near.shape
    width = 2 * count * columns
    return pl.pallas_call(
        proj_kernel,
        in_specs=[pl.BlockSpec(memory_space=pltpu.SMEM)] + [resident] * (3 + len(held)),
        out_specs=[resident, resident, resident],
        out_shape=(
            pltpu.VMEM((rows, width), bf16),
            pltpu.VMEM((rows, width), bf16),
            jax.ShapeDtypeStruct((width, depth), bf16),
        ),
        compiler_params=params(),
        cost_estimate=cost(2 * rows * depth * width, 2 * rows * depth),
    )(order, pinned(images), near, far, *map(pinned, held))


def pair_tile(tea, emb, texts, grads_ref, target=None):
    stu = texts[:, -emb.shape[1] :]
    if target is None:
        target = lax.dot_general(tea, texts[:, : tea.shape[1]], NT, preferred_element_type=f32)
        target = jnp.tanh(target + half_bias)
    student = lax.dot_general(emb, stu, NT, preferred_element_type=f32)
    coef = (jnp.tanh(student + half_bias) - target).astype(bf16)
    part = jnp.dot(coef, stu, preferred_element_type=f32)
    grads_ref[...] += lax.dot_general(coef, emb, TN, preferred_element_type=f32)
    return part


def own_kernel(target_ref, emb_ref, low_ref, high_ref, _tea_ref, out_ref, grads_ref, texts_ref):
    width = emb_ref.shape[1]
    half = low_ref.shape[0]
    texts_ref[pl.ds(0, half), :] = low_ref[:, -width:]
    texts_ref[pl.ds(half, half), :] = high_ref[:, -width:]
    size = emb_ref.shape[0]
    chunk = math.gcd(size, 512)
    grads_ref[...] = jnp.zeros_like(grads_ref)
    for k in range(size // chunk):
        rows = pl.ds(k * chunk, chunk)
        out_ref[rows, :] = pair_tile(None, emb_ref[rows, :], texts_ref, grads_ref, target_ref[rows, :])


def own_texts(target, emb, low, high, tea_emb):
    rows, width = emb.shape
    size = target.shape[1]
    return pl.pallas_call(
        own_kernel,
        in_specs=[resident] * 5,
        out_specs=[resident, resident],
        out_shape=(pltpu.VMEM((rows, width), f32), jax.ShapeDtypeStruct((size, width), f32)),
        scratch_shapes=[pltpu.VMEM((size, width), bf16)],
        compiler_params=params(),
        cost_estimate=cost(6 * rows * size * width, 6 * size * width),
    )(pinned(target), pinned(emb), low, high, pinned(tea_emb))


def join(text_refs, out_ref):
    start = 0
    for ref in text_refs:
        out_ref[pl.ds(start, ref.shape[0]), :] = ref[...]
        start += ref.shape[0]


def early_kernel(count, *refs):
    tea_ref, emb_ref = refs[:2]
    text_refs = refs[2 : 2 + count]
    before_ref, out_ref, *sum_refs, grads_ref, texts_ref = refs[2 + count :]
    size = tea_ref.shape[0]
    chunk = math.gcd(size, 512)
    join(text_refs, texts_ref)
    grads_ref[...] = jnp.zeros_like(grads_ref)
    for k in range(size // chunk):
        rows = pl.ds(k * chunk, chunk)
        part = pair_tile(tea_ref[rows, :], emb_ref[rows, :], texts_ref, grads_ref)
        out_ref[rows, :] = part + before_ref[rows, :]
    share = grads_ref.shape[0] // len(sum_refs)
    for k, ref in enumerate(sum_refs):
        ref[...] = grads_ref[pl.ds(k * share, share), :].astype(bf16)


def early(tea_emb, emb, texts, before, share):
    rows = tea_emb.shape[0]
    emb_width = emb.shape[1]
    width = texts[0].shape[1]
    count = len(texts)
    size = sum(part.shape[0] for part in texts)
    given = [pinned(tea_emb), pinned(emb), *texts, pinned(before)]
    return pl.pallas_call(
        functools.partial(early_kernel, count),
        in_specs=[resident] * len(given),
        out_specs=[resident] * (1 + size // share),
        out_shape=[pltpu.VMEM((rows, emb_width), f32)]
        + [jax.ShapeDtypeStruct((share, emb_width), bf16)] * (size // share),
        input_output_aliases={len(given) - 1: 0},
        scratch_shapes=[pltpu.VMEM((size, emb_width), f32), pltpu.VMEM((size, width), bf16)],
        compiler_params=params(4 * size * width + 4 * size * emb_width),
        cost_estimate=cost(2 * rows * size * (width + 2 * emb_width), 2 * size * (width + 2 * emb_width)),
    )(*given)


def late_kernel(count, masks, summed, order_ref, *refs):
    tea_ref, emb_ref, proj_ref, before_ref = refs[:4]
    text_refs = refs[4 : 4 + count]
    refs = refs[4 + count :]
    if summed:
        texts_before_ref, refs = refs[0], refs[1:]
    give_ref, *keep_refs, out_ref, grads_ref, texts_ref = refs
    share = keep_refs[0].shape[0]
    join(text_refs, texts_ref)
    grads_ref[...] = texts_before_ref[...] if summed else jnp.zeros_like(grads_ref)
    for k in range(masks):
        blocks = [pl.ds(pl.multiple_of(order_ref[2 * k + place] * share, share), share) for place in range(2)]
        joined = [jnp.concatenate([ref[rows, :] for rows in blocks]) for ref in (tea_ref, emb_ref)]
        grads = pair_tile(*joined, texts_ref, grads_ref)
        for place, rows in enumerate(blocks):
            whole = grads[place * share : (place + 1) * share] + before_ref[rows, :]
            floats = proj_ref[rows, :].astype(f32)
            inverse = inverse_length(floats)
            unit = floats * inverse
            along = jnp.sum(unit * whole, axis=1, keepdims=True)
            part = ((whole - unit * along) * inverse).astype(bf16)
            if place == 0:
                give_ref[pl.ds(k * share, share), :] = part
            else:
                keep_refs[k][...] = part
    out_ref[...] = grads_ref[...].astype(out_ref.dtype)


def late(order, tea_emb, emb, proj, before, texts, texts_before, share):
    tea_width, emb_width = tea_emb.shape[1], emb.shape[1]
    width = texts[0].shape[1]
    count = len(texts)
    size = sum(part.shape[0] for part in texts)
    masks = order.shape[0] // 2
    summed = texts_before is not None
    given = [pinned(tea_emb), pinned(emb), pinned(proj), pinned(before), *texts]
    given += [texts_before] if summed else []
    return pl.pallas_call(
        functools.partial(late_kernel, count, masks, summed),
        in_specs=[pl.BlockSpec(memory_space=pltpu.SMEM)] + [resident] * len(given),
        out_specs=[resident] * (masks + 2),
        out_shape=[jax.ShapeDtypeStruct((masks * share, emb_width), bf16)]
        + [jax.ShapeDtypeStruct((share, emb_width), bf16)] * masks
        + [jax.ShapeDtypeStruct((size, emb_width), bf16)],
        scratch_shapes=[pltpu.VMEM((size, emb_width), f32), pltpu.VMEM((size, width), bf16)],
        compiler_params=params(),
        cost_estimate=cost(
            4 * masks * share * size * (width + 2 * emb_width), 4 * masks * share * emb_width
        ),
    )(order, *given)


def head_kernel(order_ref, images_ref, take_ref, *refs):
    count = (len(refs) - 3) // 2
    keep_refs, (near_ref, far_ref), part_refs, total_ref = refs[:count], refs[count : count + 2], refs[count + 2 : -1], refs[-1]
    _, dp_count, rows, _ = near_ref.shape
    columns = dp_count * rows
    share = keep_refs[0].shape[0]
    total = None
    for k in range(count):
        places = pl.ds(pl.multiple_of(order_ref[2 * k] * share, share), share)
        part = keep_refs[k][...] + take_ref[pl.ds((count - 1 - k) * share, share), :]
        part_refs[k][...] = part
        term = lax.dot_general(part, images_ref[places, :], TN, preferred_element_type=f32)
        total = term if total is None else total + term
    total_ref[...] = total
    for k in range(count):
        for place, ref in enumerate((near_ref, far_ref)):
            start = pl.multiple_of(order_ref[2 * k + place] * columns, columns)
            block = total_ref[pl.ds(start, columns), :]
            for j in range(dp_count):
                ref[k, j, :, :] = block[j * rows : (j + 1) * rows].astype(bf16)


def head_parts(order, images, take, keeps, columns, dp_count):
    share, width = keeps[0].shape
    depth = images.shape[1]
    count = len(keeps)
    piece = jax.ShapeDtypeStruct((count, dp_count, columns // dp_count, depth), bf16)
    return pl.pallas_call(
        head_kernel,
        in_specs=[pl.BlockSpec(memory_space=pltpu.SMEM)] + [resident] * (2 + count),
        out_specs=[resident] * (2 + count),
        out_shape=[piece] * 2 + [jax.ShapeDtypeStruct((share, width), bf16)] * count,
        scratch_shapes=[pltpu.VMEM((width, depth), f32)],
        compiler_params=params(),
        cost_estimate=cost(2 * count * share * width * depth, 4 * count * share * width),
    )(order, pinned(images), take, *keeps)


def split_kernel(gates, order_ref, near_ref, far_ref, *refs):
    for k, ref in enumerate(refs[gates:]):
        for j in range(near_ref.shape[0]):
            ref[j, :, :] = near_ref[j, order_ref[k]] + far_ref[j, order_ref[k]]


def split(order, near, far, gates):
    count, dp_count, rows, depth = near.shape
    return pl.pallas_call(
        functools.partial(split_kernel, len(gates)),
        in_specs=[pl.BlockSpec(memory_space=pltpu.SMEM)]
        + [resident] * 2
        + [pl.BlockSpec(memory_space=pl.ANY)] * len(gates),
        out_specs=[resident] * dp_count,
        out_shape=[jax.ShapeDtypeStruct((count, rows, depth), bf16)] * dp_count,
        compiler_params=params(),
        cost_estimate=cost(0, 0),
    )(order, near, far, *gates)


def head_result_kernel(scale, order_ref, *refs):
    pieces, (out_ref, total_ref) = refs[:-2], refs[-2:]
    for k, ref in enumerate(pieces):
        total_ref[order_ref[k]] = ref[...].astype(f32)
    rows = total_ref.shape[1]
    total = jnp.concatenate([total_ref[k] for k in range(len(pieces))])
    out_ref[...] = total * scale


def head_result(order, pieces, scale):
    rows, depth = pieces[0].shape
    count = len(pieces)
    return pl.pallas_call(
        functools.partial(head_result_kernel, scale),
        in_specs=[pl.BlockSpec(memory_space=pltpu.SMEM)] + [resident] * count,
        out_specs=resident,
        out_shape=jax.ShapeDtypeStruct((count * rows, depth), f32),
        scratch_shapes=[pltpu.VMEM((count, rows, depth), f32)],
        compiler_params=params(),
        cost_estimate=cost(0, 0),
    )(order, *pieces)


def text_result_kernel(scale, stu_ref, own_ref, *refs):
    total = own_ref[...]
    for ref in refs[:-1]:
        total += ref[...].astype(f32)
    stu = stu_ref[...].astype(f32)
    inverse = inverse_length(stu)
    unit = stu * inverse
    along = jnp.sum(unit * total, axis=1, keepdims=True)
    refs[-1][...] = (total - unit * along) * (inverse * scale)


def text_result(stu_txt, own, got, scale):
    rows, width = own.shape
    return pl.pallas_call(
        functools.partial(text_result_kernel, scale),
        out_shape=jax.ShapeDtypeStruct((rows, width), f32),
        compiler_params=params(),
        cost_estimate=cost(0, 0),
    )(stu_txt, own, *got)


def images_kernel(scale, *refs):
    part_refs, head_ref, out_ref, mark_ref = refs[:-3], *refs[-3:]
    total = part_refs[0][...].astype(f32)
    for ref in part_refs[1:]:
        total += ref[...].astype(f32)
    out_ref[...] = scale * jnp.dot(total.astype(bf16), head_ref[...], preferred_element_type=f32)
    mark_ref[...] = jnp.zeros_like(mark_ref)


def image_grads(parts, head, scale):
    share, width = parts[0].shape
    depth = head.shape[1]
    return pl.pallas_call(
        functools.partial(images_kernel, scale),
        out_shape=(jax.ShapeDtypeStruct((share, depth), f32), jax.ShapeDtypeStruct((8, 128), f32)),
        compiler_params=params(),
        cost_estimate=cost(0, 0),
    )(*parts, head)


def per_device(images, head, tea_img, stu_txt, tea_txt):
    dp_count = lax.axis_size("dp")
    tensor_count = lax.axis_size("tensor")
    rank = lax.axis_index("tensor")
    rows = images.shape[0]
    columns = head.shape[1]
    share = rows // tensor_count
    half = share // 2
    pairs = tensor_count // 2
    bits = dp_count.bit_length() - 1
    factor = 0.5 * logit_scale * loss_scale / (rows * dp_count)

    texts = {0: text_halves(tea_txt, stu_txt)}
    for mask in sorted(range(1, dp_count), key=lambda m: (m.bit_count(), m)):
        first, last = mask & -mask, 1 << (mask.bit_length() - 1)
        texts[mask] = [swap(texts[mask ^ last][0], "dp", last), swap(texts[mask ^ first][1], "dp", first)]

    head_t = head.T
    tea_emb, target, held_images = teacher_emb(tea_img, images, *texts[0])
    near = stacked([head_t] + [swap(head_t, "tensor", 2 * k) for k in range(1, pairs)])
    far = swap(near, "tensor", 1)
    order = jnp.stack([rank ^ (2 * k + place) for k in range(pairs) for place in range(2)]).astype(jnp.int32)
    proj, emb, head_full = projections(order, held_images, near, far, tea_emb, target)

    text_grads = {}
    image_part, text_grads[0] = own_texts(target, emb, *texts[0], tea_emb)
    middle = list(range(1, dp_count - 1))
    given = [part for mask in middle for part in texts[mask]]
    image_part, *block_sums = early(tea_emb, emb, given, image_part, share)
    text_grads.update(zip(middle, block_sums))
    last = dp_count - 1
    chosen = jnp.stack([order[2 * k + place] for k in range(pairs)[::-1] for place in (1, 0)])
    give, *keeps, grads = late(chosen, tea_emb, emb, proj, image_part, texts[last], None, share)
    keeps = dict(zip(range(pairs)[::-1], keeps))
    take = swap(give, "tensor", 1)
    text_grads[last] = grads

    near, far, *parts = head_parts(order, held_images, take, [keeps[mask] for mask in range(pairs)], columns, dp_count)
    parts = dict(enumerate(parts))
    far = swap(far, "tensor", 1)
    dp_order = jnp.stack([lax.axis_index("dp") ^ mask for mask in range(dp_count)]).astype(jnp.int32)
    pieces = split(dp_order, near, far, [])
    pieces = [pieces[0]] + [swap(pieces[mask], "dp", mask) for mask in range(1, dp_count)]

    for bit in range(pairs.bit_length() - 1):
        sent = [mask for mask in sorted(parts) if mask >> bit & 1 and mask != 1 << bit]
        passed = [swap(parts.pop(mask), "tensor", 2 << bit) for mask in sent]
        targets = [mask ^ 1 << bit for mask in sent]
        if targets:
            parts.update(zip(targets, sums([[parts[mask], block] for mask, block in zip(targets, passed)], [far])))
    leaving = sums([[text_grads[mask]] for mask in range(1, dp_count)], [parts[pairs // 2]])
    got = {mask: swap(block, "dp", mask) for mask, block in zip(range(1, dp_count), leaving)}
    arrived = [swap(parts[1 << bit], "tensor", 2 << bit) for bit in range(pairs.bit_length() - 1)]
    grad_images, images_mark = image_grads([parts[0]] + arrived, head_full, factor)

    held, count = pieces, pairs
    while count > 1:
        low, high = folded(held)
        held = [low, swap(high, "tensor", count)]
        count //= 2
    (own,) = sums([held], arrived)
    own = own[0]
    shares = [own] + [swap(own, "dp", mask) for mask in range(1, dp_count)]
    grad_head = head_result(dp_order, shares, factor).T

    grad_text = text_result(stu_txt, text_grads[0], list(got.values()), factor / half_scale)
    return (grad_images, grad_head, grad_text)


def solution(mesh):
    placed = (
        P("dp", None),
        P(None, "tensor"),
        P("dp", None),
        P(("dp", "tensor"), None),
        P(("dp", "tensor"), None),
    )
    return jax.shard_map(
        per_device,
        mesh=mesh,
        in_specs=placed,
        out_specs=(P(("dp", "tensor"), None), P(None, "tensor"), P(("dp", "tensor"), None)),
        check_vma=False,
    )
```

```python
import functools
import math
import jax
import jax.numpy as jnp
from jax import lax
from jax.experimental import pallas as pl
from jax.experimental.pallas import tpu as pltpu
from jax.sharding import PartitionSpec as P

logit_scale = 64.0
logit_bias = -2.0
loss_scale = 65536.0
half_scale = 0.5 * logit_scale
half_bias = 0.5 * logit_bias
bf16 = jnp.bfloat16
f32 = jnp.float32
NT = (((1,), (1,)), ((), ()))
TN = (((0,), (0,)), ((), ()))


def params(held=0):
    return pltpu.CompilerParams(vmem_limit_bytes=held + 10 * 1024 * 1024)


resident = pl.BlockSpec(memory_space=pltpu.VMEM)


def pinned(value):
    return pltpu.with_memory_space_constraint(value, pltpu.VMEM)


def cost(flops, moved, trans=0):
    return pl.CostEstimate(flops=int(flops), bytes_accessed=int(moved), transcendentals=int(trans))


def swap(value, axis, mask):
    count = lax.axis_size(axis)
    return lax.ppermute(value, axis, [(source, source ^ mask) for source in range(count)])


def inverse_length(floats):
    return lax.rsqrt(jnp.sum(floats * floats, axis=1, keepdims=True) + 1e-06)


def in_hbm(value):
    return pltpu.with_memory_space_constraint(value, pltpu.HBM)


def stack_kernel(*refs):
    piece_refs, out_ref = refs[:-1], refs[-1]
    for k, ref in enumerate(piece_refs):
        out_ref[k, :, :] = ref[...]


def stacked(pieces):
    shape = (len(pieces), *pieces[0].shape)
    return pl.pallas_call(
        stack_kernel,
        in_specs=[resident] * len(pieces),
        out_specs=resident,
        out_shape=jax.ShapeDtypeStruct(shape, pieces[0].dtype),
        compiler_params=params(),
        cost_estimate=cost(0, 4 * math.prod(shape)),
    )(*pieces)


def sum_kernel(groups, *refs):
    start = 0
    for terms, out_ref in zip(groups, refs[-len(groups) :]):
        total = refs[start][...].astype(f32)
        for ref in refs[start + 1 : start + terms]:
            total += ref[...].astype(f32)
        out_ref[...] = total.astype(bf16)
        start += terms


def sums(groups, gates):
    given = [term for group in groups for term in group]
    size = sum(math.prod(term.shape) for term in given)
    return pl.pallas_call(
        functools.partial(sum_kernel, [len(group) for group in groups]),
        in_specs=[resident] * len(given) + [pl.BlockSpec(memory_space=pl.ANY)] * len(gates),
        out_specs=[resident] * len(groups),
        out_shape=[jax.ShapeDtypeStruct(group[0].shape, bf16) for group in groups],
        compiler_params=params(),
        cost_estimate=cost(0, 0),
    )(*given, *gates)


def fold_kernel(*refs):
    terms, (low_ref, high_ref) = refs[:-2], refs[-2:]
    half = low_ref.shape[0]
    for k, out_ref in enumerate((low_ref, high_ref)):
        total = terms[0][k * half : (k + 1) * half].astype(f32)
        for ref in terms[1:]:
            total += ref[k * half : (k + 1) * half].astype(f32)
        out_ref[...] = total.astype(bf16)


def folded(terms):
    count, *rest = terms[0].shape
    size = len(terms) * math.prod(terms[0].shape)
    return pl.pallas_call(
        fold_kernel,
        in_specs=[resident] * len(terms),
        out_specs=[resident] * 2,
        out_shape=[jax.ShapeDtypeStruct((count // 2, *rest), bf16)] * 2,
        compiler_params=params(),
        cost_estimate=cost(0, 0),
    )(*terms)


def text_kernel(tea_ref, stu_ref, low_ref, high_ref):
    tea_width = tea_ref.shape[1]
    for place, out_ref in enumerate((low_ref, high_ref)):

        @pl.when(pl.program_id(0) == place)
        def _(out_ref=out_ref):
            tea = tea_ref[...].astype(f32)
            out_ref[:, :tea_width] = (tea * inverse_length(tea)).astype(bf16)
            stu = stu_ref[...].astype(f32)
            out_ref[:, tea_width:] = (stu * inverse_length(stu)).astype(bf16)


def text_halves(tea_txt, stu_txt):
    share, tea_width = tea_txt.shape
    stu_width = stu_txt.shape[1]
    half = share // 2
    part = jax.ShapeDtypeStruct((half, tea_width + stu_width), bf16)
    row = lambda width: pl.BlockSpec((half, width), lambda i: (i, 0))
    return pl.pallas_call(
        text_kernel,
        grid=(2,),
        in_specs=[row(tea_width), row(stu_width)],
        out_specs=[resident] * 2,
        out_shape=(part, part),
        compiler_params=params(),
        cost_estimate=cost(4 * share * tea_width, 4 * share * tea_width),
    )(in_hbm(tea_txt), in_hbm(stu_txt))


def teacher_kernel(tea_ref, images_ref, low_ref, high_ref, emb_ref, target_ref, held_ref):
    chunk, width = tea_ref.shape
    rows = pl.ds(pl.multiple_of(pl.program_id(0) * chunk, chunk), chunk)
    tea = tea_ref[...].astype(f32)
    emb = (tea * inverse_length(tea)).astype(bf16) * half_scale
    emb_ref[rows, :] = emb
    half = low_ref.shape[0]
    for place, ref in enumerate((low_ref, high_ref)):
        target = lax.dot_general(emb, ref[:, :width], NT, preferred_element_type=f32)
        target_ref[rows, pl.ds(place * half, half)] = jnp.tanh(target + half_bias)
    held_ref[rows, :] = images_ref[...]


def teacher_emb(tea_img, images, low, high):
    rows, width = tea_img.shape
    depth = images.shape[1]
    chunk = math.gcd(rows, 512)
    size = 2 * low.shape[0]
    row = lambda width: pl.BlockSpec((chunk, width), lambda i: (i, 0))
    return pl.pallas_call(
        teacher_kernel,
        grid=(rows // chunk,),
        in_specs=[row(width), row(depth), resident, resident],
        out_specs=[resident] * 3,
        out_shape=(
            pltpu.VMEM((rows, width), bf16),
            pltpu.VMEM((rows, size), f32),
            pltpu.VMEM((rows, depth), bf16),
        ),
        compiler_params=params(),
        cost_estimate=cost(2 * rows * width * size, 2 * rows * width),
    )(in_hbm(tea_img), in_hbm(images), low, high)


def proj_kernel(order_ref, images_ref, near_ref, far_ref, _tea_ref, _target_ref, proj_ref, emb_ref, head_ref):
    count, columns = near_ref.shape[:2]
    size = images_ref.shape[0]
    chunk = math.gcd(size, 512)
    for k in range(count):
        for place, ref in enumerate((near_ref, far_ref)):
            start = pl.multiple_of(order_ref[2 * k + place] * columns, columns)
            head_ref[pl.ds(start, columns), :] = ref[k]
    for k in range(size // chunk):
        rows = pl.ds(k * chunk, chunk)
        proj = lax.dot_general(images_ref[rows, :], head_ref[...], NT, preferred_element_type=f32).astype(bf16)
        floats = proj.astype(f32)
        proj_ref[rows, :] = proj
        emb_ref[rows, :] = (floats * inverse_length(floats)).astype(bf16) * half_scale


def projections(order, images, near, far, *held):
    rows, depth = images.shape
    count, columns, _ = near.shape
    width = 2 * count * columns
    return pl.pallas_call(
        proj_kernel,
        in_specs=[pl.BlockSpec(memory_space=pltpu.SMEM)] + [resident] * (3 + len(held)),
        out_specs=[resident, resident, resident],
        out_shape=(
            pltpu.VMEM((rows, width), bf16),
            pltpu.VMEM((rows, width), bf16),
            jax.ShapeDtypeStruct((width, depth), bf16),
        ),
        compiler_params=params(),
        cost_estimate=cost(2 * rows * depth * width, 2 * rows * depth),
    )(order, pinned(images), near, far, *map(pinned, held))


def pair_tile(tea, emb, texts, grads_ref, target=None):
    stu = texts[:, -emb.shape[1] :]
    if target is None:
        target = lax.dot_general(tea, texts[:, : tea.shape[1]], NT, preferred_element_type=f32)
        target = jnp.tanh(target + half_bias)
    student = lax.dot_general(emb, stu, NT, preferred_element_type=f32)
    coef = (jnp.tanh(student + half_bias) - target).astype(bf16)
    part = jnp.dot(coef, stu, preferred_element_type=f32)
    grads_ref[...] += lax.dot_general(coef, emb, TN, preferred_element_type=f32)
    return part


def own_kernel(target_ref, emb_ref, low_ref, high_ref, _tea_ref, out_ref, grads_ref, texts_ref):
    width = emb_ref.shape[1]
    half = low_ref.shape[0]
    texts_ref[pl.ds(0, half), :] = low_ref[:, -width:]
    texts_ref[pl.ds(half, half), :] = high_ref[:, -width:]
    size = emb_ref.shape[0]
    chunk = math.gcd(size, 512)
    grads_ref[...] = jnp.zeros_like(grads_ref)
    for k in range(size // chunk):
        rows = pl.ds(k * chunk, chunk)
        out_ref[rows, :] = pair_tile(None, emb_ref[rows, :], texts_ref, grads_ref, target_ref[rows, :])


def own_texts(target, emb, low, high, tea_emb):
    rows, width = emb.shape
    size = target.shape[1]
    return pl.pallas_call(
        own_kernel,
        in_specs=[resident] * 5,
        out_specs=[resident, resident],
        out_shape=(pltpu.VMEM((rows, width), f32), jax.ShapeDtypeStruct((size, width), f32)),
        scratch_shapes=[pltpu.VMEM((size, width), bf16)],
        compiler_params=params(),
        cost_estimate=cost(6 * rows * size * width, 6 * size * width),
    )(pinned(target), pinned(emb), low, high, pinned(tea_emb))


def join(text_refs, out_ref):
    start = 0
    for ref in text_refs:
        out_ref[pl.ds(start, ref.shape[0]), :] = ref[...]
        start += ref.shape[0]


def early_kernel(count, *refs):
    tea_ref, emb_ref = refs[:2]
    text_refs = refs[2 : 2 + count]
    before_ref, out_ref, *sum_refs, grads_ref, texts_ref = refs[2 + count :]
    size = tea_ref.shape[0]
    chunk = math.gcd(size, 512)
    join(text_refs, texts_ref)
    grads_ref[...] = jnp.zeros_like(grads_ref)
    for k in range(size // chunk):
        rows = pl.ds(k * chunk, chunk)
        part = pair_tile(tea_ref[rows, :], emb_ref[rows, :], texts_ref, grads_ref)
        out_ref[rows, :] = part + before_ref[rows, :]
    share = grads_ref.shape[0] // len(sum_refs)
    for k, ref in enumerate(sum_refs):
        ref[...] = grads_ref[pl.ds(k * share, share), :].astype(bf16)


def early(tea_emb, emb, texts, before, share):
    rows = tea_emb.shape[0]
    emb_width = emb.shape[1]
    width = texts[0].shape[1]
    count = len(texts)
    size = sum(part.shape[0] for part in texts)
    given = [pinned(tea_emb), pinned(emb), *texts, pinned(before)]
    return pl.pallas_call(
        functools.partial(early_kernel, count),
        in_specs=[resident] * len(given),
        out_specs=[resident] * (1 + size // share),
        out_shape=[pltpu.VMEM((rows, emb_width), f32)]
        + [pltpu.VMEM((share, emb_width), bf16)] * (size // share),
        input_output_aliases={len(given) - 1: 0},
        scratch_shapes=[pltpu.VMEM((size, emb_width), f32), pltpu.VMEM((size, width), bf16)],
        compiler_params=params(4 * size * width + 4 * size * emb_width),
        cost_estimate=cost(2 * rows * size * (width + 2 * emb_width), 2 * size * (width + 2 * emb_width)),
    )(*given)


def late_kernel(count, masks, summed, order_ref, *refs):
    tea_ref, emb_ref, proj_ref, before_ref = refs[:4]
    text_refs = refs[4 : 4 + count]
    refs = refs[4 + count :]
    if summed:
        texts_before_ref, refs = refs[0], refs[1:]
    give_ref, *keep_refs, out_ref, grads_ref, texts_ref = refs
    share = keep_refs[0].shape[0]
    join(text_refs, texts_ref)
    grads_ref[...] = texts_before_ref[...] if summed else jnp.zeros_like(grads_ref)
    for k in range(masks):
        blocks = [pl.ds(pl.multiple_of(order_ref[2 * k + place] * share, share), share) for place in range(2)]
        joined = [jnp.concatenate([ref[rows, :] for rows in blocks]) for ref in (tea_ref, emb_ref)]
        grads = pair_tile(*joined, texts_ref, grads_ref)
        for place, rows in enumerate(blocks):
            whole = grads[place * share : (place + 1) * share] + before_ref[rows, :]
            floats = proj_ref[rows, :].astype(f32)
            inverse = inverse_length(floats)
            unit = floats * inverse
            along = jnp.sum(unit * whole, axis=1, keepdims=True)
            part = ((whole - unit * along) * inverse).astype(bf16)
            if place == 0:
                give_ref[pl.ds(k * share, share), :] = part
            else:
                keep_refs[k][...] = part
    out_ref[...] = grads_ref[...].astype(out_ref.dtype)


def late(order, tea_emb, emb, proj, before, texts, texts_before, share):
    tea_width, emb_width = tea_emb.shape[1], emb.shape[1]
    width = texts[0].shape[1]
    count = len(texts)
    size = sum(part.shape[0] for part in texts)
    masks = order.shape[0] // 2
    summed = texts_before is not None
    given = [pinned(tea_emb), pinned(emb), pinned(proj), pinned(before), *texts]
    given += [texts_before] if summed else []
    return pl.pallas_call(
        functools.partial(late_kernel, count, masks, summed),
        in_specs=[pl.BlockSpec(memory_space=pltpu.SMEM)] + [resident] * len(given),
        out_specs=[resident] * (masks + 2),
        out_shape=[jax.ShapeDtypeStruct((masks * share, emb_width), bf16)]
        + [jax.ShapeDtypeStruct((share, emb_width), bf16)] * masks
        + [jax.ShapeDtypeStruct((size, emb_width), bf16)],
        scratch_shapes=[pltpu.VMEM((size, emb_width), f32), pltpu.VMEM((size, width), bf16)],
        compiler_params=params(),
        cost_estimate=cost(
            4 * masks * share * size * (width + 2 * emb_width), 4 * masks * share * emb_width
        ),
    )(order, *given)


def head_kernel(order_ref, images_ref, take_ref, *refs):
    count = (len(refs) - 3) // 2
    keep_refs, (near_ref, far_ref), part_refs, total_ref = refs[:count], refs[count : count + 2], refs[count + 2 : -1], refs[-1]
    _, dp_count, rows, _ = near_ref.shape
    columns = dp_count * rows
    share = keep_refs[0].shape[0]
    total = None
    for k in range(count):
        places = pl.ds(pl.multiple_of(order_ref[2 * k] * share, share), share)
        part = keep_refs[k][...] + take_ref[pl.ds((count - 1 - k) * share, share), :]
        part_refs[k][...] = part
        term = lax.dot_general(part, images_ref[places, :], TN, preferred_element_type=f32)
        total = term if total is None else total + term
    total_ref[...] = total
    for k in range(count):
        for place, ref in enumerate((near_ref, far_ref)):
            start = pl.multiple_of(order_ref[2 * k + place] * columns, columns)
            block = total_ref[pl.ds(start, columns), :]
            for j in range(dp_count):
                ref[k, j, :, :] = block[j * rows : (j + 1) * rows].astype(bf16)


def head_parts(order, images, take, keeps, columns, dp_count):
    share, width = keeps[0].shape
    depth = images.shape[1]
    count = len(keeps)
    piece = jax.ShapeDtypeStruct((count, dp_count, columns // dp_count, depth), bf16)
    return pl.pallas_call(
        head_kernel,
        in_specs=[pl.BlockSpec(memory_space=pltpu.SMEM)] + [resident] * (2 + count),
        out_specs=[resident] * (2 + count),
        out_shape=[piece] * 2 + [jax.ShapeDtypeStruct((share, width), bf16)] * count,
        scratch_shapes=[pltpu.VMEM((width, depth), f32)],
        compiler_params=params(),
        cost_estimate=cost(2 * count * share * width * depth, 4 * count * share * width),
    )(order, pinned(images), take, *keeps)


def split_kernel(gates, order_ref, near_ref, far_ref, *refs):
    for k, ref in enumerate(refs[gates:]):
        for j in range(near_ref.shape[0]):
            ref[j, :, :] = near_ref[j, order_ref[k]] + far_ref[j, order_ref[k]]


def split(order, near, far, gates):
    count, dp_count, rows, depth = near.shape
    return pl.pallas_call(
        functools.partial(split_kernel, len(gates)),
        in_specs=[pl.BlockSpec(memory_space=pltpu.SMEM)]
        + [resident] * 2
        + [pl.BlockSpec(memory_space=pl.ANY)] * len(gates),
        out_specs=[resident] * dp_count,
        out_shape=[jax.ShapeDtypeStruct((count, rows, depth), bf16)] * dp_count,
        compiler_params=params(),
        cost_estimate=cost(0, 0),
    )(order, near, far, *gates)


def head_result_kernel(scale, order_ref, *refs):
    pieces, (out_ref, total_ref) = refs[:-2], refs[-2:]
    for k, ref in enumerate(pieces):
        total_ref[order_ref[k]] = ref[...].astype(f32)
    rows = total_ref.shape[1]
    total = jnp.concatenate([total_ref[k] for k in range(len(pieces))])
    out_ref[...] = total * scale


def head_result(order, pieces, scale):
    rows, depth = pieces[0].shape
    count = len(pieces)
    return pl.pallas_call(
        functools.partial(head_result_kernel, scale),
        in_specs=[pl.BlockSpec(memory_space=pltpu.SMEM)] + [resident] * count,
        out_specs=resident,
        out_shape=jax.ShapeDtypeStruct((count * rows, depth), f32),
        scratch_shapes=[pltpu.VMEM((count, rows, depth), f32)],
        compiler_params=params(),
        cost_estimate=cost(0, 0),
    )(order, *pieces)


def text_result_kernel(scale, stu_ref, own_ref, *refs):
    total = own_ref[...]
    for ref in refs[:-1]:
        total += ref[...].astype(f32)
    stu = stu_ref[...].astype(f32)
    inverse = inverse_length(stu)
    unit = stu * inverse
    along = jnp.sum(unit * total, axis=1, keepdims=True)
    refs[-1][...] = (total - unit * along) * (inverse * scale)


def text_result(stu_txt, own, got, scale):
    rows, width = own.shape
    return pl.pallas_call(
        functools.partial(text_result_kernel, scale),
        out_shape=jax.ShapeDtypeStruct((rows, width), f32),
        compiler_params=params(),
        cost_estimate=cost(0, 0),
    )(stu_txt, own, *got)


def images_kernel(scale, *refs):
    part_refs, head_ref, out_ref, mark_ref = refs[:-3], *refs[-3:]
    total = part_refs[0][...].astype(f32)
    for ref in part_refs[1:]:
        total += ref[...].astype(f32)
    out_ref[...] = scale * jnp.dot(total.astype(bf16), head_ref[...], preferred_element_type=f32)
    mark_ref[...] = jnp.zeros_like(mark_ref)


def image_grads(parts, head, scale):
    share, width = parts[0].shape
    depth = head.shape[1]
    return pl.pallas_call(
        functools.partial(images_kernel, scale),
        out_shape=(jax.ShapeDtypeStruct((share, depth), f32), jax.ShapeDtypeStruct((8, 128), f32)),
        compiler_params=params(),
        cost_estimate=cost(0, 0),
    )(*parts, head)


def per_device(images, head, tea_img, stu_txt, tea_txt):
    dp_count = lax.axis_size("dp")
    tensor_count = lax.axis_size("tensor")
    rank = lax.axis_index("tensor")
    rows = images.shape[0]
    columns = head.shape[1]
    share = rows // tensor_count
    half = share // 2
    pairs = tensor_count // 2
    bits = dp_count.bit_length() - 1
    factor = 0.5 * logit_scale * loss_scale / (rows * dp_count)

    texts = {0: text_halves(tea_txt, stu_txt)}
    for mask in sorted(range(1, dp_count), key=lambda m: (m.bit_count(), m)):
        first, last = mask & -mask, 1 << (mask.bit_length() - 1)
        texts[mask] = [swap(texts[mask ^ last][0], "dp", last), swap(texts[mask ^ first][1], "dp", first)]

    head_t = head.T
    tea_emb, target, held_images = teacher_emb(tea_img, images, *texts[0])
    near = stacked([head_t] + [swap(head_t, "tensor", 2 * k) for k in range(1, pairs)])
    far = swap(near, "tensor", 1)
    order = jnp.stack([rank ^ (2 * k + place) for k in range(pairs) for place in range(2)]).astype(jnp.int32)
    proj, emb, head_full = projections(order, held_images, near, far, tea_emb, target)

    text_grads = {}
    image_part, text_grads[0] = own_texts(target, emb, *texts[0], tea_emb)
    middle = list(range(1, dp_count - 1))
    given = [part for mask in middle for part in texts[mask]]
    image_part, *block_sums = early(tea_emb, emb, given, image_part, share)
    text_grads.update(zip(middle, block_sums))
    last = dp_count - 1
    chosen = jnp.stack([order[2 * k + place] for k in range(pairs)[::-1] for place in (1, 0)])
    give, *keeps, grads = late(chosen, tea_emb, emb, proj, image_part, texts[last], None, share)
    keeps = dict(zip(range(pairs)[::-1], keeps))
    take = swap(give, "tensor", 1)
    text_grads[last] = grads

    near, far, *parts = head_parts(order, held_images, take, [keeps[mask] for mask in range(pairs)], columns, dp_count)
    parts = dict(enumerate(parts))
    far = swap(far, "tensor", 1)
    dp_order = jnp.stack([lax.axis_index("dp") ^ mask for mask in range(dp_count)]).astype(jnp.int32)
    pieces = split(dp_order, near, far, [])
    pieces = [pieces[0]] + [swap(pieces[mask], "dp", mask) for mask in range(1, dp_count)]

    for bit in range(pairs.bit_length() - 1):
        sent = [mask for mask in sorted(parts) if mask >> bit & 1 and mask != 1 << bit]
        passed = [swap(parts.pop(mask), "tensor", 2 << bit) for mask in sent]
        targets = [mask ^ 1 << bit for mask in sent]
        if targets:
            parts.update(zip(targets, sums([[parts[mask], block] for mask, block in zip(targets, passed)], [far])))
    leaving = sums([[pinned(text_grads[mask]) if mask in middle else text_grads[mask]] for mask in range(1, dp_count)], [parts[pairs // 2]])
    got = {mask: swap(block, "dp", mask) for mask, block in zip(range(1, dp_count), leaving)}
    arrived = [swap(parts[1 << bit], "tensor", 2 << bit) for bit in range(pairs.bit_length() - 1)]
    grad_images, images_mark = image_grads([parts[0]] + arrived, head_full, factor)

    held, count = pieces, pairs
    while count > 1:
        low, high = folded(held)
        held = [low, swap(high, "tensor", count)]
        count //= 2
    (own,) = sums([held], arrived)
    own = own[0]
    shares = [own] + [swap(own, "dp", mask) for mask in range(1, dp_count)]
    grad_head = head_result(dp_order, shares, factor).T

    grad_text = text_result(stu_txt, text_grads[0], list(got.values()), factor / half_scale)
    return (grad_images, grad_head, grad_text)


def solution(mesh):
    placed = (
        P("dp", None),
        P(None, "tensor"),
        P("dp", None),
        P(("dp", "tensor"), None),
        P(("dp", "tensor"), None),
    )
    return jax.shard_map(
        per_device,
        mesh=mesh,
        in_specs=placed,
        out_specs=(P(("dp", "tensor"), None), P(None, "tensor"), P(("dp", "tensor"), None)),
        check_vma=False,
    )
```
